32 devices in a mesh: gossip: 8 (over z, x), fsdp: 4 (over y, core).
Axes of the slice: x: 2, y: 2, z: 4, core: 2. Of those that a mesh axis runs over, the one named last changes fastest.
Arguments:
- inputs: bfloat16 [8, 2048, 2048], P('gossip', 'fsdp'), may hold values from -6 to 6
- out_grad: bfloat16 [8, 2048, 2048], P('gossip', 'fsdp'), may hold values from -6 to 6
- norm_gain: float32 [8, 2048], P('gossip'), may hold values from 0.5 to 1.5
- w_qkv: bfloat16 [8, 16, 2048, 384], P('gossip', 'fsdp'), may hold values from -64 to 64
- w_out: bfloat16 [8, 16, 128, 2048], P('gossip', 'fsdp'), may hold values from -6 to 6
- mom_qkv: bfloat16 [8, 16, 2048, 384], P('gossip', 'fsdp'), may hold values from -6 to 6
- mom_out: bfloat16 [8, 16, 128, 2048], P('gossip', 'fsdp'), may hold values from -6 to 6
- step_index: int32 [1], replicated, may hold values from 0 to 11
Outputs:
- new_qkv: bfloat16 [8, 16, 2048, 384], P('gossip', 'fsdp')
- new_out: bfloat16 [8, 16, 128, 2048], P('gossip', 'fsdp')
- new_mom_qkv: bfloat16 [8, 16, 2048, 384], P('gossip', 'fsdp')
- new_mom_out: bfloat16 [8, 16, 128, 2048], P('gossip', 'fsdp')
The draws below stay inside these ranges and needn't reach their ends.
All inputs are finite; a program needn't handle non-finite values.
Results may differ from the reference program's by a relative error of at most 0.0085.
Values may be sent and summed in bfloat16 or wider, within the bound.
No kernel may reach another device: no remote copies, remote signals or barrier semaphores. Data moves between devices by JAX's collectives and lax.ppermute only.
A program may use at most 192 MiB of HBM per device.

```python
import math
import jax
import jax.numpy as jnp
from jax import lax

D = 2048
HEADS = 16
HD = 128
SEQ = 2048
LEVELS = 3
N_GOSSIP = 8


def draw_w_qkv(key, part):
    first_key = jax.random.fold_in(jax.random.fold_in(key, 11), 0)
    base = jnp.clip(jax.random.normal(first_key, (N_GOSSIP, HEADS, D, 3 * HD), jnp.float32), -6.0, 6.0)
    return base.astype(jnp.bfloat16)


def block_levels(key, extent, cuts, least, top_value):
    level, own = 1.0, jax.random.fold_in(key, 6)
    for dim, shards_of in cuts:
        heights = jnp.exp(jax.random.uniform(jax.random.fold_in(own, dim), (shards_of,), jnp.float32, least / len(cuts), top_value / len(cuts)))
        level = level * jnp.repeat(heights, extent[dim] // shards_of).reshape([-1 if axis == dim else 1 for axis in range(len(extent))])
    return level


def gaussian(rng, shape, deviation, limit, cuts=(), held_as=jnp.bfloat16):
    result = deviation * jax.random.normal(rng, shape, jnp.float32)
    if cuts:
        result = result * block_levels(rng, shape, cuts, -0.22, 0.18)
    return jnp.clip(result, -limit, limit).astype(held_as)


def setup_inputs(seed: int = 0) -> dict:
    keys = jax.random.split(jax.random.key(seed), 9)
    return {
        "inputs": gaussian(keys[0], (N_GOSSIP, SEQ, D), 1.0, 6.0, ((0, 8), (1, 4))),
        "out_grad": gaussian(keys[1], (N_GOSSIP, SEQ, D), 1.0, 6.0, ((0, 8), (1, 4))),
        "norm_gain": jnp.clip(1.0 + 0.1 * jax.random.normal(keys[2], (N_GOSSIP, D), jnp.float32), 0.5, 1.5),
        "w_qkv": draw_w_qkv(jax.random.fold_in(keys[8], 71), 0),
        "w_out": gaussian(keys[4], (N_GOSSIP, HEADS, HD, D), 1.0, 6.0, ((0, 8), (1, 4))),
        "mom_qkv": gaussian(keys[5], (N_GOSSIP, HEADS, D, 3 * HD), 1.0, 6.0, ((0, 8), (1, 4))),
        "mom_out": gaussian(keys[6], (N_GOSSIP, HEADS, HD, D), 1.0, 6.0, ((0, 8), (1, 4))),
        "step_index": jax.random.randint(keys[7], (1,), 0, 4 * LEVELS).astype(jnp.int32),
    }


BETA = 0.9
RATE = 0.1
EPSILON = 1e-05

def rotate(tensor, positions):
    half_width = tensor.shape[-1] // 2
    frequency = jnp.exp(-math.log(10000.0) * 2.0 * jnp.arange(half_width, dtype=jnp.float32) / tensor.shape[-1])
    angles = positions.astype(jnp.float32)[:, None] * frequency[None, :]
    cosine = jnp.cos(angles)
    sine_vals = jnp.sin(angles)
    first = tensor[..., :half_width]
    second = tensor[..., half_width:]
    return jnp.concatenate([first * cosine - second * sine_vals, second * cosine + first * sine_vals], -1)

def unrotate(grad_in, positions):
    half_width = grad_in.shape[-1] // 2
    frequency = jnp.exp(-math.log(10000.0) * 2.0 * jnp.arange(half_width, dtype=jnp.float32) / grad_in.shape[-1])
    angles = positions.astype(jnp.float32)[:, None] * frequency[None, :]
    cosine = jnp.cos(angles)
    sine_vals = jnp.sin(angles)
    first = grad_in[..., :half_width]
    second = grad_in[..., half_width:]
    return jnp.concatenate([first * cosine + second * sine_vals, second * cosine - first * sine_vals], -1)

def attend(queries, key_rows, val_rows):
    seq_len, head_dim = queries.shape
    block_len = min(512, seq_len)
    scale = 1.0 / math.sqrt(head_dim)
    outputs = []
    prob_list = []
    for block_num in range(seq_len // block_len):
        begin = block_num * block_len
        key_end = begin + block_len
        scores = jnp.dot(queries[begin:key_end], key_rows[:key_end].T, preferred_element_type=jnp.float32) * scale
        row_pos = begin + jnp.arange(block_len)[:, None]
        col_pos = jnp.arange(key_end)[None, :]
        scores = jnp.where(col_pos <= row_pos, scores, -jnp.inf)
        top = lax.optimization_barrier(jnp.max(scores, -1, keepdims=True))
        weights = jnp.exp(scores - top)
        weights = weights / lax.optimization_barrier(jnp.sum(weights, -1, keepdims=True))
        prob_list.append(weights)
        outputs.append(jnp.dot(weights.astype(jnp.bfloat16), val_rows[:key_end], preferred_element_type=jnp.float32))
    return (jnp.concatenate(outputs, 0).astype(jnp.bfloat16), prob_list)

def attend_back(queries, key_rows, val_rows, prob_list, grad_att):
    seq_len, head_dim = queries.shape
    block_len = min(512, seq_len)
    scale = 1.0 / math.sqrt(head_dim)
    grad_q_list = []
    grad_keys = jnp.zeros((seq_len, head_dim), jnp.float32)
    grad_vals = jnp.zeros((seq_len, head_dim), jnp.float32)
    for block_num in range(seq_len // block_len):
        begin = block_num * block_len
        key_end = begin + block_len
        weights = prob_list[block_num]
        weights_b = weights.astype(jnp.bfloat16)
        grad_block = grad_att[begin:key_end]
        grad_probs = jnp.dot(grad_block, val_rows[:key_end].T, preferred_element_type=jnp.float32)
        centred = grad_probs - lax.optimization_barrier(jnp.sum(weights * grad_probs, -1, keepdims=True))
        grad_scores = (weights * centred * scale).astype(jnp.bfloat16)
        grad_q_list.append(jnp.dot(grad_scores, key_rows[:key_end], preferred_element_type=jnp.float32))
        grad_keys = grad_keys.at[:key_end].add(jnp.dot(grad_scores.T, queries[begin:key_end], preferred_element_type=jnp.float32))
        grad_vals = grad_vals.at[:key_end].add(jnp.dot(weights_b.T, grad_block, preferred_element_type=jnp.float32))
    return (jnp.concatenate(grad_q_list, 0), grad_keys, grad_vals)

def advance(weight, moment, gradient, rate):
    moved_m = (BETA * moment.astype(jnp.float32) + gradient.astype(jnp.float32)).astype(jnp.bfloat16)
    moved_w = (weight.astype(jnp.float32) - rate * moved_m.astype(jnp.float32)).astype(jnp.bfloat16)
    return (moved_w, moved_m)

def replica_update(packed, rate):
    rows, grad_rows, gain_row, weight_qkv, weight_out, moment_qkv, moment_out = packed
    rows_f = rows.astype(jnp.float32)
    stats = lax.rsqrt(lax.optimization_barrier(jnp.mean(rows_f * rows_f, -1, keepdims=True)) + EPSILON)
    normed = (rows_f * stats * gain_row[None, :]).astype(jnp.bfloat16)
    seq_len, width = normed.shape
    head_dim = weight_out.shape[1]
    positions = jnp.arange(seq_len)
    out_scale = 1.0 / math.sqrt(HEADS * head_dim)

    def per_head(head_pair):
        head_qkv, head_out = head_pair
        projected = jnp.dot(normed, head_qkv, preferred_element_type=jnp.float32) * (1.0 / math.sqrt(width))
        queries = rotate(projected[:, :head_dim], positions).astype(jnp.bfloat16)
        key_rows = rotate(projected[:, head_dim:2 * head_dim], positions).astype(jnp.bfloat16)
        val_rows = projected[:, 2 * head_dim:].astype(jnp.bfloat16)
        attended, prob_list = attend(queries, key_rows, val_rows)
        grad_out = (jnp.dot(attended.T, grad_rows, preferred_element_type=jnp.float32) * out_scale).astype(jnp.bfloat16)
        grad_att = (jnp.dot(grad_rows, head_out.T, preferred_element_type=jnp.float32) * out_scale).astype(jnp.bfloat16)
        grad_q, grad_k, grad_v = attend_back(queries, key_rows, val_rows, prob_list, grad_att)
        grad_proj = jnp.concatenate([unrotate(grad_q, positions), unrotate(grad_k, positions), grad_v], -1)
        grad_proj = (grad_proj * (1.0 / math.sqrt(width))).astype(jnp.bfloat16)
        grad_qkv = jnp.dot(normed.T, grad_proj, preferred_element_type=jnp.float32).astype(jnp.bfloat16)
        return (grad_qkv, grad_out)
    grad_qkv, grad_out = lax.map(per_head, (weight_qkv, weight_out))
    moved_qkv, moved_mqkv = advance(weight_qkv, moment_qkv, grad_qkv, rate)
    moved_out, moved_mout = advance(weight_out, moment_out, grad_out, rate)
    return (moved_qkv, moved_out, moved_mqkv, moved_mout)

def reference(inputs, out_grad, norm_gain, w_qkv, w_out, mom_qkv, mom_out, step_index):
    rate = RATE * (step_index[0].astype(jnp.float32) + 1.0) / (4.0 * LEVELS)
    moved = lax.map(lambda packed: replica_update(packed, rate), (inputs, out_grad, norm_gain, w_qkv, w_out, mom_qkv, mom_out))
    exponent = jnp.remainder(step_index[0].astype(jnp.int32), jnp.int32(LEVELS)).astype(jnp.int32)
    distance = jnp.left_shift(jnp.int32(1), exponent)
    results = []
    for own in moved:
        partner = jnp.roll(own, distance, axis=0)
        results.append(((own.astype(jnp.float32) + partner.astype(jnp.float32)) * 0.5).astype(jnp.bfloat16))
    return (results[0], results[1], results[2], results[3])
```

```python
from functools import partial
import math

import jax
import jax.numpy as jnp
from jax import lax
from jax.experimental import pallas as pl
from jax.experimental.pallas import tpu as pltpu
from jax.sharding import PartitionSpec as P

HEADS = 16
LEVELS = 3

BETA = 0.9
RATE = 0.1
EPSILON = 1e-05

VMEM_LIMIT = 48 * 1024 * 1024
BLOCK = 256


def product(left, right, left_dim=1, right_dim=0):
    return lax.dot_general(
        left, right, (((left_dim,), (right_dim,)), ((), ())), preferred_element_type=jnp.float32
    )


def params():
    return pltpu.CompilerParams(vmem_limit_bytes=VMEM_LIMIT)


def shifted(value, by):
    size = lax.axis_size("gossip")
    return lax.ppermute(value, "gossip", [(i, (i + by) % size) for i in range(size)])


def rotary_tables(seq_len, head_dim):
    half = head_dim // 2
    frequency = jnp.exp(
        -math.log(10000.0) * 2.0 * jnp.arange(half, dtype=jnp.float32) / head_dim
    )
    angles = jnp.arange(seq_len).astype(jnp.float32)[:, None] * frequency[None, :]
    return jnp.cos(angles), jnp.sin(angles)


def project_kernel(scale, rows_ref, weight_ref, cos_ref, sin_ref, q_ref, k_ref, v_ref):
    rows = rows_ref[...]
    cosine, sine = cos_ref[...], sin_ref[...]
    width = cosine.shape[-1]
    for head in range(weight_ref.shape[0]):
        projected = product(rows, weight_ref[head]) * scale
        for which, out_ref in enumerate((q_ref, k_ref)):
            part = projected[:, which * width : (which + 1) * width]
            turned = part * cosine + pltpu.roll(part, width // 2, 1) * sine
            out_ref[head] = turned.astype(jnp.bfloat16)
        v_ref[head] = projected[:, 2 * width :].astype(jnp.bfloat16)


def project(rows, weights, cosine, sine):
    seq_len, width = rows.shape
    heads, _, three = weights.shape
    head_dim = three // 3
    block = min(BLOCK, seq_len)
    out = jax.ShapeDtypeStruct((heads, seq_len, head_dim), jnp.bfloat16)
    out_spec = pl.BlockSpec((heads, block, head_dim), lambda i: (0, i, 0))
    return pl.pallas_call(
        partial(project_kernel, 1.0 / math.sqrt(width)),
        grid=(seq_len // block,),
        in_specs=[
            pl.BlockSpec((block, width), lambda i: (i, 0)),
            pl.BlockSpec((heads, width, three), lambda i: (0, 0, 0)),
            pl.BlockSpec((block, head_dim), lambda i: (i, 0)),
            pl.BlockSpec((block, head_dim), lambda i: (i, 0)),
        ],
        out_specs=[out_spec] * 3,
        out_shape=[out] * 3,
        compiler_params=params(),
        cost_estimate=pl.CostEstimate(
            flops=2 * seq_len * width * heads * three,
            bytes_accessed=2 * (rows.size + weights.size + seq_len * heads * three),
            transcendentals=0,
        ),
        name="project",
    )(rows, weights, cosine, sine)


def cotangent_kernel(scale, rows_ref, weight_ref, out_ref):
    rows = rows_ref[...]
    for head in range(weight_ref.shape[0]):
        out_ref[head] = (product(rows, weight_ref[head], 1, 1) * scale).astype(jnp.bfloat16)


def cotangent(rows, weights, scale):
    seq_len, width = rows.shape
    heads, head_dim, _ = weights.shape
    block = min(2 * BLOCK, seq_len)
    return pl.pallas_call(
        partial(cotangent_kernel, scale),
        grid=(seq_len // block,),
        in_specs=[
            pl.BlockSpec((block, width), lambda i: (i, 0)),
            pl.BlockSpec((heads, head_dim, width), lambda i: (0, 0, 0)),
        ],
        out_specs=pl.BlockSpec((heads, block, head_dim), lambda i: (0, i, 0)),
        out_shape=jax.ShapeDtypeStruct((heads, seq_len, head_dim), jnp.bfloat16),
        compiler_params=params(),
        cost_estimate=pl.CostEstimate(
            flops=2 * seq_len * width * heads * head_dim,
            bytes_accessed=2 * (rows.size + weights.size + seq_len * heads * head_dim),
            transcendentals=0,
        ),
        name="cotangent",
    )(rows, weights)


def folded(values, combine):
    rows, columns = values.shape
    return combine(values.reshape(rows // 8, 8, columns), 0)


def attention_kernel(
    scale,
    proj_scale,
    q_ref,
    k_ref,
    v_ref,
    g_ref,
    cos_ref,
    sin_ref,
    grad_ref,
    att_ref,
    s_ref,
    p_ref,
    d_ref,
    kt_ref,
    vt_ref,
    gk_ref,
    gv_ref,
):
    step = pl.program_id(0)
    block = s_ref.shape[1]
    head_dim = q_ref.shape[-1]
    half = head_dim // 2

    here = pl.ds(pl.multiple_of(step * block, block), block)
    queries = q_ref[0, here, :]
    grads = g_ref[0, here, :]
    kt_ref[step] = k_ref[0, here, :].T
    vt_ref[step] = v_ref[0, here, :].T
    gk_ref[step] = jnp.zeros(gk_ref.shape[1:], jnp.float32)
    gv_ref[step] = jnp.zeros(gv_ref.shape[1:], jnp.float32)

    def rows(tile):
        return pl.ds(pl.multiple_of(tile * block, block), block)

    scores = product(k_ref[0, here, :], queries, 1, 1)
    key_pos = lax.broadcasted_iota(jnp.int32, scores.shape, 0)
    query_pos = lax.broadcasted_iota(jnp.int32, scores.shape, 1)
    scores = jnp.where(key_pos <= query_pos, scores, -jnp.inf)
    s_ref[step] = scores

    def score(tile, top):
        scores = product(k_ref[0, rows(tile), :], queries, 1, 1)
        s_ref[tile] = scores
        return jnp.maximum(top, folded(scores, jnp.max))

    top = lax.fori_loop(0, step, score, folded(scores, jnp.max))
    factor = scale * math.log2(math.e)
    top = jnp.max(top, 0, keepdims=True) * factor

    def weigh(tile, sums):
        total, inner = sums
        weights = jnp.exp2(s_ref[tile] * factor - top)
        grad_probs = product(v_ref[0, rows(tile), :], grads, 1, 1)
        p_ref[tile] = weights
        d_ref[tile] = grad_probs
        return total + folded(weights, jnp.sum), inner + folded(weights * grad_probs, jnp.sum)

    zeros = jnp.zeros((8, block), jnp.float32)
    total, inner = lax.fori_loop(0, step + 1, weigh, (zeros, zeros))
    inverse = 1.0 / jnp.sum(total, 0, keepdims=True)
    inner = jnp.sum(inner, 0, keepdims=True) * inverse

    def back(tile, sums):
        att, grad_q = sums
        probs = p_ref[tile] * inverse
        probs_b = probs.astype(jnp.bfloat16)
        grad_scores = (probs * (d_ref[tile] - inner)).astype(jnp.bfloat16)
        gv_ref[tile] += product(probs_b, grads)
        gk_ref[tile] += product(grad_scores, queries)
        return att + product(vt_ref[tile], probs_b), grad_q + product(kt_ref[tile], grad_scores)

    zeros = jnp.zeros((head_dim, block), jnp.float32)
    att, grad_q = lax.fori_loop(0, step + 1, back, (zeros, zeros))

    def unrotate(grad, where):
        cosine, sine = cos_ref[:, where], sin_ref[:, where]
        first, second = grad[:half], grad[half:]
        factor = scale * proj_scale
        return (
            ((first * cosine + second * sine) * factor).astype(jnp.bfloat16),
            ((second * cosine - first * sine) * factor).astype(jnp.bfloat16),
        )

    att_ref[:, here] = att.astype(jnp.bfloat16)
    first, second = unrotate(grad_q, here)
    grad_ref[:half, here] = first
    grad_ref[half:head_dim, here] = second

    @pl.when(step == pl.num_programs(0) - 1)
    def finish():
        def keys(tile, carry):
            where = rows(tile)
            first, second = unrotate(gk_ref[tile].T, where)
            grad_ref[head_dim : head_dim + half, where] = first
            grad_ref[head_dim + half : 2 * head_dim, where] = second
            values = gv_ref[tile].T * proj_scale
            grad_ref[2 * head_dim :, where] = values.astype(jnp.bfloat16)
            return carry

        lax.fori_loop(0, pl.num_programs(0), keys, 0)


def attention(head, queries, keys, values, grads, cosine_t, sine_t, width):
    _, seq_len, head_dim = queries.shape
    block = min(BLOCK, seq_len)
    tiles = seq_len // block
    of_head = pl.BlockSpec((1, seq_len, head_dim), lambda i: (head, 0, 0))
    whole = pl.BlockSpec((head_dim // 2, seq_len), lambda i: (0, 0))
    pairs = seq_len * (seq_len + block) // 2
    return pl.pallas_call(
        partial(attention_kernel, 1.0 / math.sqrt(head_dim), 1.0 / math.sqrt(width)),
        grid=(tiles,),
        in_specs=[of_head] * 4 + [whole] * 2,
        out_specs=[
            pl.BlockSpec((3 * head_dim, seq_len), lambda i: (0, 0)),
            pl.BlockSpec((head_dim, seq_len), lambda i: (0, 0)),
        ],
        out_shape=[
            jax.ShapeDtypeStruct((3 * head_dim, seq_len), jnp.bfloat16),
            jax.ShapeDtypeStruct((head_dim, seq_len), jnp.bfloat16),
        ],
        scratch_shapes=[pltpu.VMEM((tiles, block, block), jnp.float32)] * 3
        + [pltpu.VMEM((tiles, head_dim, block), jnp.bfloat16)] * 2
        + [pltpu.VMEM((tiles, block, head_dim), jnp.float32)] * 2,
        compiler_params=params(),
        cost_estimate=pl.CostEstimate(
            flops=12 * pairs * head_dim,
            bytes_accessed=2 * 8 * seq_len * head_dim,
            transcendentals=pairs,
        ),
        name="attention",
    )(queries, keys, values, grads, cosine_t, sine_t)


def momenta_kernel(
    scale, grad_ref, att_ref, normed_ref, rows_ref, mqkv_ref, mout_ref, moved_ref, moved_out_ref
):
    grad = product(grad_ref[...], normed_ref[...]).T.astype(jnp.bfloat16)
    moved = BETA * mqkv_ref[0].astype(jnp.float32) + grad.astype(jnp.float32)
    moved_ref[...] = moved.astype(jnp.bfloat16)
    grad = (product(att_ref[...], rows_ref[...]) * scale).astype(jnp.bfloat16)
    moved = BETA * mout_ref[0].astype(jnp.float32) + grad.astype(jnp.float32)
    moved_out_ref[...] = moved.astype(jnp.bfloat16)


def momenta(head, grad_proj, attended, normed, rows, mom_qkv, mom_out, scale):
    seq_len, width = normed.shape
    three, head_dim = grad_proj.shape[0], attended.shape[0]
    block = min(BLOCK, width)
    return pl.pallas_call(
        partial(momenta_kernel, scale),
        grid=(width // block,),
        in_specs=[
            pl.BlockSpec((three, seq_len), lambda i: (0, 0)),
            pl.BlockSpec((head_dim, seq_len), lambda i: (0, 0)),
            pl.BlockSpec((seq_len, block), lambda i: (0, i)),
            pl.BlockSpec((seq_len, block), lambda i: (0, i)),
            pl.BlockSpec((1, block, three), lambda i: (head, i, 0)),
            pl.BlockSpec((1, head_dim, block), lambda i: (head, 0, i)),
        ],
        out_specs=[
            pl.BlockSpec((block, three), lambda i: (i, 0)),
            pl.BlockSpec((head_dim, block), lambda i: (0, i)),
        ],
        out_shape=[
            jax.ShapeDtypeStruct((width, three), jnp.bfloat16),
            jax.ShapeDtypeStruct((head_dim, width), jnp.bfloat16),
        ],
        compiler_params=params(),
        cost_estimate=pl.CostEstimate(
            flops=2 * seq_len * width * (three + head_dim),
            bytes_accessed=2 * (2 * seq_len * width + 3 * width * (three + head_dim)),
            transcendentals=0,
        ),
        name="momenta",
    )(grad_proj, attended, normed, rows, mom_qkv, mom_out)


def average_kernel(rate_ref, *refs):
    rate = rate_ref[0, 0]
    outs = refs[-4:]

    def halfway(own, other):
        return ((own.astype(jnp.float32) + other.astype(jnp.float32)) * 0.5).astype(jnp.bfloat16)

    def moved(weight, moment):
        new = weight.astype(jnp.float32) - rate * moment.astype(jnp.float32)
        return new.astype(jnp.bfloat16)

    for part in range(2):
        weight, other_weight, moment, other_moment = (r for r in refs[4 * part : 4 * part + 4])
        own_m, other_m = moment[...], other_moment[...]
        own_w = moved(weight[0], own_m)
        other_w = moved(other_weight[0], other_m)
        outs[part][0] = halfway(own_w, other_w)
        outs[2 + part][0] = halfway(own_m, other_m)


def average(head, rate, own, other, moments, other_moments, previous):
    heads = own[0].shape[0]
    steps = 4
    in_specs = [pl.BlockSpec(memory_space=pltpu.SMEM)]
    args = [rate]
    out_specs, out_shape = [], []
    for part in range(2):
        _, high, wide = own[part].shape
        stacked = pl.BlockSpec((1, high // steps, wide), lambda i: (head, i, 0))
        single = pl.BlockSpec((high // steps, wide), lambda i: (i, 0))
        in_specs += [stacked, stacked, single, single]
        args += [own[part], other[part], moments[part], other_moments[part]]
        out_specs.append(stacked)
        out_shape.append(jax.ShapeDtypeStruct((heads, high, wide), jnp.bfloat16))
    aliases = {}
    if previous is not None:
        aliases = {len(args) + i: i for i in range(4)}
        args += list(previous)
        in_specs += [pl.BlockSpec(memory_space=pl.ANY)] * 4
    return pl.pallas_call(
        average_kernel,
        grid=(steps,),
        in_specs=in_specs,
        out_specs=out_specs * 2,
        out_shape=out_shape * 2,
        input_output_aliases=aliases,
        compiler_params=params(),
        cost_estimate=pl.CostEstimate(
            flops=10 * sum(m.size for m in moments),
            bytes_accessed=12 * sum(m.size for m in moments),
            transcendentals=0,
        ),
        name="average",
    )(*args)


def update(by, inputs, out_grad, norm_gain, w_qkv, w_out, mom_qkv, mom_out, rate):
    own = (w_qkv, w_out)
    other = tuple(shifted(w, by) for w in own)

    rows_f = inputs.astype(jnp.float32)
    stats = lax.rsqrt(jnp.mean(rows_f * rows_f, -1, keepdims=True) + EPSILON)
    normed = (rows_f * stats * norm_gain[None, :]).astype(jnp.bfloat16)
    normed = lax.all_gather(normed, "fsdp", axis=0, tiled=True)
    rows = lax.all_gather(out_grad, "fsdp", axis=0, tiled=True)

    seq_len, width = normed.shape
    heads, head_dim, _ = w_out.shape
    out_scale = 1.0 / math.sqrt(HEADS * head_dim)
    cosine, sine = rotary_tables(seq_len, head_dim)
    queries, keys, values = project(
        normed,
        w_qkv,
        jnp.concatenate([cosine, cosine], -1),
        jnp.concatenate([-sine, sine], -1),
    )
    grads = cotangent(rows, w_out, out_scale)
    moments, other_moments = [], []
    for head in range(heads):
        grad_proj, attended = attention(
            head, queries, keys, values, grads, cosine.T, sine.T, width
        )
        moved = momenta(head, grad_proj, attended, normed, rows, mom_qkv, mom_out, out_scale)
        moments.append(moved)
        other_moments.append([shifted(m, by) for m in moved])
    results = None
    for head in range(heads):
        results = average(head, rate, own, other, moments[head], other_moments[head], results)
    return tuple(results)


def per_device(inputs, out_grad, norm_gain, w_qkv, w_out, mom_qkv, mom_out, step_index):
    rate = RATE * (step_index[0].astype(jnp.float32) + 1.0) / (4.0 * LEVELS)
    exponent = jnp.remainder(step_index[0], LEVELS)
    results = lax.switch(
        exponent,
        [partial(update, 1 << level) for level in range(LEVELS)],
        inputs[0],
        out_grad[0],
        norm_gain[0],
        w_qkv[0],
        w_out[0],
        mom_qkv[0],
        mom_out[0],
        rate.reshape(1, 1),
    )
    return tuple(r[None] for r in results)


def solution(mesh):
    return jax.shard_map(
        per_device,
        mesh=mesh,
        in_specs=(
            P("gossip", "fsdp", None),
            P("gossip", "fsdp", None),
            P("gossip", None),
            P("gossip", "fsdp", None, None),
            P("gossip", "fsdp", None, None),
            P("gossip", "fsdp", None, None),
            P("gossip", "fsdp", None, None),
            P(),
        ),
        out_specs=(
            P("gossip", "fsdp", None, None),
            P("gossip", "fsdp", None, None),
            P("gossip", "fsdp", None, None),
            P("gossip", "fsdp", None, None),
        ),
        check_vma=False,
    )
```

```python
from functools import partial
import math

import jax
import jax.numpy as jnp
from jax import lax
from jax.experimental import pallas as pl
from jax.experimental.pallas import tpu as pltpu
from jax.sharding import PartitionSpec as P

HEADS = 16
LEVELS = 3

BETA = 0.9
RATE = 0.1
EPSILON = 1e-05

VMEM_LIMIT = 63 * 1024 * 1024
BLOCK = 512

SHORT = pl.CostEstimate(flops=1, bytes_accessed=1, transcendentals=0)


def product(left, right, left_dim=1, right_dim=0):
    return lax.dot_general(
        left, right, (((left_dim,), (right_dim,)), ((), ())), preferred_element_type=jnp.float32
    )


def params():
    return pltpu.CompilerParams(vmem_limit_bytes=VMEM_LIMIT)


def shifted(value, by):
    size = lax.axis_size("gossip")
    return lax.ppermute(value, "gossip", [(i, (i + by) % size) for i in range(size)])


def rotary_tables(seq_len, head_dim):
    half = head_dim // 2
    frequency = jnp.exp(
        -math.log(10000.0) * 2.0 * jnp.arange(half, dtype=jnp.float32) / head_dim
    )
    angles = jnp.arange(seq_len).astype(jnp.float32)[:, None] * frequency[None, :]
    return jnp.cos(angles), jnp.sin(angles)


def project_kernel(scale, rows_ref, weight_ref, cos_ref, sin_ref, q_ref, k_ref, v_ref):
    cosine, sine = cos_ref[...], sin_ref[...]
    width = cosine.shape[-1]
    projected = product(rows_ref[...], weight_ref[0]) * scale
    for which, out_ref in enumerate((q_ref, k_ref)):
        part = projected[:, which * width : (which + 1) * width]
        turned = part * cosine + pltpu.roll(part, width // 2, 1) * sine
        out_ref[...] = turned.astype(jnp.bfloat16)
    v_ref[...] = projected[:, 2 * width :].astype(jnp.bfloat16)


def project(head, rows, weights, cosine, sine):
    seq_len, width = rows.shape
    three = weights.shape[-1]
    head_dim = three // 3
    block = min(BLOCK, seq_len)
    out = jax.ShapeDtypeStruct((seq_len, head_dim), jnp.bfloat16)
    out_spec = pl.BlockSpec((block, head_dim), lambda i: (i, 0))
    return pl.pallas_call(
        partial(project_kernel, 1.0 / math.sqrt(width)),
        grid=(seq_len // block,),
        in_specs=[
            pl.BlockSpec((block, width), lambda i: (i, 0)),
            pl.BlockSpec((1, width, three), lambda i: (head, 0, 0)),
            out_spec,
            out_spec,
        ],
        out_specs=[out_spec] * 3,
        out_shape=[out] * 3,
        compiler_params=params(),
        cost_estimate=SHORT,
        name="project",
    )(rows, weights, cosine, sine)


def cotangent_kernel(scale, rows_ref, weight_ref, out_ref):
    rows = rows_ref[...]
    for head in range(weight_ref.shape[0]):
        out_ref[head] = (product(rows, weight_ref[head], 1, 1) * scale).astype(jnp.bfloat16)


def cotangent(rows, weights, scale):
    seq_len, width = rows.shape
    heads, head_dim, _ = weights.shape
    block = min(BLOCK, seq_len)
    return pl.pallas_call(
        partial(cotangent_kernel, scale),
        grid=(seq_len // block,),
        in_specs=[
            pl.BlockSpec((block, width), lambda i: (i, 0)),
            pl.BlockSpec((heads, head_dim, width), lambda i: (0, 0, 0)),
        ],
        out_specs=pl.BlockSpec((heads, block, head_dim), lambda i: (0, i, 0)),
        out_shape=jax.ShapeDtypeStruct((heads, seq_len, head_dim), jnp.bfloat16),
        compiler_params=params(),
        cost_estimate=SHORT,
        name="cotangent",
    )(rows, weights)


def folded(values, combine):
    rows, columns = values.shape
    return combine(values.reshape(rows // 8, 8, columns), 0)


def attention_kernel(
    scale,
    proj_scale,
    q_ref,
    k_ref,
    v_ref,
    g_ref,
    cos_ref,
    sin_ref,
    grad_ref,
    att_ref,
    s_ref,
    p_ref,
    d_ref,
    kt_ref,
    vt_ref,
    gk_ref,
    gv_ref,
):
    step = pl.program_id(0)
    block = s_ref.shape[1]
    head_dim = q_ref.shape[-1]
    half = head_dim // 2

    here = pl.ds(pl.multiple_of(step * block, block), block)
    queries = q_ref[here, :]
    grads = g_ref[0, here, :]
    kt_ref[step] = k_ref[here, :].T
    vt_ref[step] = v_ref[here, :].T
    gk_ref[step] = jnp.zeros(gk_ref.shape[1:], jnp.float32)
    gv_ref[step] = jnp.zeros(gv_ref.shape[1:], jnp.float32)

    def rows(tile):
        return pl.ds(pl.multiple_of(tile * block, block), block)

    scores = product(k_ref[here, :], queries, 1, 1)
    key_pos = lax.broadcasted_iota(jnp.int32, scores.shape, 0)
    query_pos = lax.broadcasted_iota(jnp.int32, scores.shape, 1)
    scores = jnp.where(key_pos <= query_pos, scores, -jnp.inf)
    s_ref[step] = scores

    def score(tile, top):
        scores = product(k_ref[rows(tile), :], queries, 1, 1)
        s_ref[tile] = scores
        return jnp.maximum(top, folded(scores, jnp.max))

    top = lax.fori_loop(0, step, score, folded(scores, jnp.max))
    factor = scale * math.log2(math.e)
    top = jnp.max(top, 0, keepdims=True) * factor

    def weigh(tile, sums):
        total, inner = sums
        weights = jnp.exp2(s_ref[tile] * factor - top)
        grad_probs = product(v_ref[rows(tile), :], grads, 1, 1)
        p_ref[tile] = weights
        d_ref[tile] = grad_probs
        return total + folded(weights, jnp.sum), inner + folded(weights * grad_probs, jnp.sum)

    zeros = jnp.zeros((8, block), jnp.float32)
    total, inner = lax.fori_loop(0, step + 1, weigh, (zeros, zeros))
    inverse = 1.0 / jnp.sum(total, 0, keepdims=True)
    inner = jnp.sum(inner, 0, keepdims=True) * inverse

    def back(tile, sums):
        att, grad_q = sums
        probs = p_ref[tile] * inverse
        probs_b = probs.astype(jnp.bfloat16)
        grad_scores = (probs * (d_ref[tile] - inner)).astype(jnp.bfloat16)
        gv_ref[tile] += product(probs_b, grads)
        gk_ref[tile] += product(grad_scores, queries)
        return att + product(vt_ref[tile], probs_b), grad_q + product(kt_ref[tile], grad_scores)

    zeros = jnp.zeros((head_dim, block), jnp.float32)
    att, grad_q = lax.fori_loop(0, step + 1, back, (zeros, zeros))

    def unrotate(grad, where):
        cosine, sine = cos_ref[:, where], sin_ref[:, where]
        first, second = grad[:half], grad[half:]
        factor = scale * proj_scale
        return (
            ((first * cosine + second * sine) * factor).astype(jnp.bfloat16),
            ((second * cosine - first * sine) * factor).astype(jnp.bfloat16),
        )

    att_ref[:, here] = att.astype(jnp.bfloat16)
    first, second = unrotate(grad_q, here)
    grad_ref[:half, here] = first
    grad_ref[half:head_dim, here] = second

    @pl.when(step == pl.num_programs(0) - 1)
    def finish():
        def keys(tile, carry):
            where = rows(tile)
            first, second = unrotate(gk_ref[tile].T, where)
            grad_ref[head_dim : head_dim + half, where] = first
            grad_ref[head_dim + half : 2 * head_dim, where] = second
            values = gv_ref[tile].T * proj_scale
            grad_ref[2 * head_dim :, where] = values.astype(jnp.bfloat16)
            return carry

        lax.fori_loop(0, pl.num_programs(0), keys, 0)


def attention(head, queries, keys, values, grads, cosine_t, sine_t, width):
    seq_len, head_dim = queries.shape
    block = min(BLOCK, seq_len)
    tiles = seq_len // block
    of_head = pl.BlockSpec((seq_len, head_dim), lambda i: (0, 0))
    stacked = pl.BlockSpec((1, seq_len, head_dim), lambda i: (head, 0, 0))
    whole = pl.BlockSpec((head_dim // 2, seq_len), lambda i: (0, 0))
    return pl.pallas_call(
        partial(attention_kernel, 1.0 / math.sqrt(head_dim), 1.0 / math.sqrt(width)),
        grid=(tiles,),
        in_specs=[of_head] * 3 + [stacked] + [whole] * 2,
        out_specs=[
            pl.BlockSpec((3 * head_dim, seq_len), lambda i: (0, 0)),
            pl.BlockSpec((head_dim, seq_len), lambda i: (0, 0)),
        ],
        out_shape=[
            jax.ShapeDtypeStruct((3 * head_dim, seq_len), jnp.bfloat16),
            jax.ShapeDtypeStruct((head_dim, seq_len), jnp.bfloat16),
        ],
        scratch_shapes=[pltpu.VMEM((tiles, block, block), jnp.float32)] * 3
        + [pltpu.VMEM((tiles, head_dim, block), jnp.bfloat16)] * 2
        + [pltpu.VMEM((tiles, block, head_dim), jnp.float32)] * 2,
        compiler_params=params(),
        cost_estimate=SHORT,
        name="attention",
    )(queries, keys, values, grads, cosine_t, sine_t)


def momenta_kernel(
    scale, grad_ref, att_ref, normed_ref, rows_ref, mqkv_ref, mout_ref, moved_ref
):
    three = grad_ref.shape[0]
    grad = product(grad_ref[...], normed_ref[...]).T.astype(jnp.bfloat16)
    moved = BETA * mqkv_ref[0].astype(jnp.float32) + grad.astype(jnp.float32)
    moved_ref[:, :three] = moved.astype(jnp.bfloat16)
    grad = (product(att_ref[...], rows_ref[...]) * scale).astype(jnp.bfloat16)
    moved = BETA * mout_ref[0].astype(jnp.float32) + grad.astype(jnp.float32)
    moved_ref[:, three:] = moved.T.astype(jnp.bfloat16)


def momenta(head, piece, grad_proj, attended, normed, rows, mom_qkv, mom_out, scale):
    first, count, block = piece
    seq_len = normed.shape[0]
    three, head_dim = grad_proj.shape[0], attended.shape[0]
    return pl.pallas_call(
        partial(momenta_kernel, scale),
        grid=(count,),
        in_specs=[
            pl.BlockSpec((three, seq_len), lambda i: (0, 0)),
            pl.BlockSpec((head_dim, seq_len), lambda i: (0, 0)),
            pl.BlockSpec((seq_len, block), lambda i: (0, first + i)),
            pl.BlockSpec((seq_len, block), lambda i: (0, first + i)),
            pl.BlockSpec((1, block, three), lambda i: (head, first + i, 0)),
            pl.BlockSpec((1, head_dim, block), lambda i: (head, 0, first + i)),
        ],
        out_specs=pl.BlockSpec((block, three + head_dim), lambda i: (i, 0)),
        out_shape=jax.ShapeDtypeStruct((count * block, three + head_dim), jnp.bfloat16),
        compiler_params=params(),
        cost_estimate=SHORT,
        name="momenta",
    )(grad_proj, attended, normed, rows, mom_qkv, mom_out)


def average_kernel(rate_ref, qkv, other_qkv, out, other_out, moment, other_moment, *refs):
    rate = rate_ref[0, 0]
    new_qkv, new_out, new_mom_qkv, new_mom_out = refs[-4:]
    three = qkv.shape[-1]

    def halfway(own, other):
        return ((own.astype(jnp.float32) + other.astype(jnp.float32)) * 0.5).astype(jnp.bfloat16)

    def moved(weight, moment):
        new = weight.astype(jnp.float32) - rate * moment.astype(jnp.float32)
        return new.astype(jnp.bfloat16)

    own, other = moment[:, :three], other_moment[:, :three]
    new_qkv[0] = halfway(moved(qkv[0], own), moved(other_qkv[0], other))
    new_mom_qkv[0] = halfway(own, other)
    own = moment[:, three:].astype(jnp.float32).T
    other = other_moment[:, three:].astype(jnp.float32).T
    new_out[0] = halfway(moved(out[0], own), moved(other_out[0], other))
    new_mom_out[0] = halfway(own, other)


def average(head, piece, rate, own, other, moment, other_moment, previous):
    first, count, block = piece
    (qkv, out), (other_qkv, other_out) = own, other
    three, head_dim = qkv.shape[-1], out.shape[1]
    high = pl.BlockSpec((1, block, three), lambda i: (head, first + i, 0))
    wide = pl.BlockSpec((1, head_dim, block), lambda i: (head, 0, first + i))
    packed = pl.BlockSpec((block, three + head_dim), lambda i: (i, 0))
    in_specs = [pl.BlockSpec(memory_space=pltpu.SMEM), high, high, wide, wide, packed, packed]
    args = [rate, qkv, other_qkv, out, other_out, moment, other_moment]
    aliases = {}
    if previous is not None:
        aliases = {len(args) + i: i for i in range(4)}
        args += list(previous)
        in_specs += [pl.BlockSpec(memory_space=pl.ANY)] * 4
    return pl.pallas_call(
        average_kernel,
        grid=(count,),
        in_specs=in_specs,
        out_specs=[high, wide] * 2,
        out_shape=[jax.ShapeDtypeStruct(w.shape, jnp.bfloat16) for w in own] * 2,
        input_output_aliases=aliases,
        compiler_params=params(),
        cost_estimate=SHORT,
        name="average",
    )(*args)


def pieces_of(head, heads, width):
    block = min(BLOCK, width)
    blocks = width // block
    if head < heads - 1 or blocks < 4:
        return [(0, blocks, block)]
    return [(0, blocks - 2, block), (blocks - 2, 1, block), (blocks - 1, 1, block)]


def update(by, inputs, out_grad, norm_gain, w_qkv, w_out, mom_qkv, mom_out, rate):
    own = (w_qkv, w_out)
    other = tuple(shifted(w, by) for w in own)

    rows_f = inputs.astype(jnp.float32)
    stats = lax.rsqrt(jnp.mean(rows_f * rows_f, -1, keepdims=True) + EPSILON)
    normed = (rows_f * stats * norm_gain[None, :]).astype(jnp.bfloat16)
    normed = lax.all_gather(normed, "fsdp", axis=0, tiled=True)
    rows = lax.all_gather(out_grad, "fsdp", axis=0, tiled=True)

    seq_len, width = normed.shape
    heads, head_dim, _ = w_out.shape
    out_scale = 1.0 / math.sqrt(HEADS * head_dim)
    cosine, sine = rotary_tables(seq_len, head_dim)
    full_cosine = jnp.concatenate([cosine, cosine], -1)
    full_sine = jnp.concatenate([-sine, sine], -1)
    grads = cotangent(rows, w_out, out_scale)
    made = []
    for head in range(heads):
        queries, keys, values = project(head, normed, w_qkv, full_cosine, full_sine)
        grad_proj, attended = attention(
            head, queries, keys, values, grads, cosine.T, sine.T, width
        )
        for piece in pieces_of(head, heads, width):
            moment = momenta(
                head, piece, grad_proj, attended, normed, rows, mom_qkv, mom_out, out_scale
            )
            normed, moment = lax.optimization_barrier((normed, moment))
            made.append((head, piece, moment, shifted(moment, by)))
    results = None
    for head, piece, moment, other_moment in made:
        results = average(head, piece, rate, own, other, moment, other_moment, results)
    return tuple(results)


def per_device(inputs, out_grad, norm_gain, w_qkv, w_out, mom_qkv, mom_out, step_index):
    rate = RATE * (step_index[0].astype(jnp.float32) + 1.0) / (4.0 * LEVELS)
    exponent = jnp.remainder(step_index[0], LEVELS)
    results = lax.switch(
        exponent,
        [partial(update, 1 << level) for level in range(LEVELS)],
        inputs[0],
        out_grad[0],
        norm_gain[0],
        w_qkv[0],
        w_out[0],
        mom_qkv[0],
        mom_out[0],
        rate.reshape(1, 1),
    )
    return tuple(r[None] for r in results)


def solution(mesh):
    return jax.shard_map(
        per_device,
        mesh=mesh,
        in_specs=(
            P("gossip", "fsdp", None),
            P("gossip", "fsdp", None),
            P("gossip", None),
            P("gossip", "fsdp", None, None),
            P("gossip", "fsdp", None, None),
            P("gossip", "fsdp", None, None),
            P("gossip", "fsdp", None, None),
            P(),
        ),
        out_specs=(
            P("gossip", "fsdp", None, None),
            P("gossip", "fsdp", None, None),
            P("gossip", "fsdp", None, None),
            P("gossip", "fsdp", None, None),
        ),
        check_vma=False,
    )
```

```python
from functools import partial
import math

import jax
import jax.numpy as jnp
from jax import lax
from jax.experimental import pallas as pl
from jax.experimental.pallas import tpu as pltpu
from jax.sharding import PartitionSpec as P

HEADS = 16
LEVELS = 3

BETA = 0.9
RATE = 0.1
EPSILON = 1e-05

VMEM_LIMIT = 63 * 1024 * 1024
BLOCK = 512

SHORT = pl.CostEstimate(flops=1, bytes_accessed=1, transcendentals=0)


def product(left, right, left_dim=1, right_dim=0):
    return lax.dot_general(
        left, right, (((left_dim,), (right_dim,)), ((), ())), preferred_element_type=jnp.float32
    )


def params():
    return pltpu.CompilerParams(vmem_limit_bytes=VMEM_LIMIT)


def shifted(value, by):
    size = lax.axis_size("gossip")
    return lax.ppermute(value, "gossip", [(i, (i + by) % size) for i in range(size)])


def rotary_tables(seq_len, head_dim):
    half = head_dim // 2
    frequency = jnp.exp(
        -math.log(10000.0) * 2.0 * jnp.arange(half, dtype=jnp.float32) / head_dim
    )
    angles = jnp.arange(seq_len).astype(jnp.float32)[:, None] * frequency[None, :]
    return jnp.cos(angles), jnp.sin(angles)


def project_kernel(scale, rows_ref, weight_ref, cos_ref, sin_ref, q_ref, k_ref, v_ref):
    cosine, sine = cos_ref[...], sin_ref[...]
    width = cosine.shape[-1]
    projected = product(rows_ref[...], weight_ref[0]) * scale
    for which, out_ref in enumerate((q_ref, k_ref)):
        part = projected[:, which * width : (which + 1) * width]
        turned = part * cosine + pltpu.roll(part, width // 2, 1) * sine
        out_ref[...] = turned.astype(jnp.bfloat16)
    v_ref[...] = projected[:, 2 * width :].astype(jnp.bfloat16)


def project(head, rows, weights, cosine, sine):
    seq_len, width = rows.shape
    three = weights.shape[-1]
    head_dim = three // 3
    block = min(BLOCK, seq_len)
    out = jax.ShapeDtypeStruct((seq_len, head_dim), jnp.bfloat16)
    out_spec = pl.BlockSpec((block, head_dim), lambda i: (i, 0))
    return pl.pallas_call(
        partial(project_kernel, 1.0 / math.sqrt(width)),
        grid=(seq_len // block,),
        in_specs=[
            pl.BlockSpec((block, width), lambda i: (i, 0)),
            pl.BlockSpec((1, width, three), lambda i: (head, 0, 0)),
            out_spec,
            out_spec,
        ],
        out_specs=[out_spec] * 3,
        out_shape=[out] * 3,
        compiler_params=params(),
        cost_estimate=SHORT,
        name="project",
    )(rows, weights, cosine, sine)


def cotangent_kernel(scale, rows_ref, weight_ref, out_ref):
    rows = rows_ref[...]
    for head in range(weight_ref.shape[0]):
        out_ref[head] = (product(rows, weight_ref[head], 1, 1) * scale).astype(jnp.bfloat16)


def cotangent(rows, weights, scale):
    seq_len, width = rows.shape
    heads, head_dim, _ = weights.shape
    block = min(BLOCK, seq_len)
    return pl.pallas_call(
        partial(cotangent_kernel, scale),
        grid=(seq_len // block,),
        in_specs=[
            pl.BlockSpec((block, width), lambda i: (i, 0)),
            pl.BlockSpec((heads, head_dim, width), lambda i: (0, 0, 0)),
        ],
        out_specs=pl.BlockSpec((heads, block, head_dim), lambda i: (0, i, 0)),
        out_shape=jax.ShapeDtypeStruct((heads, seq_len, head_dim), jnp.bfloat16),
        compiler_params=params(),
        cost_estimate=SHORT,
        name="cotangent",
    )(rows, weights)


def folded(values, combine):
    rows, columns = values.shape
    return combine(values.reshape(rows // 8, 8, columns), 0)


def attention_kernel(
    scale,
    proj_scale,
    q_ref,
    k_ref,
    v_ref,
    g_ref,
    cos_ref,
    sin_ref,
    grad_ref,
    att_ref,
    s_ref,
    p_ref,
    d_ref,
    kt_ref,
    vt_ref,
    gk_ref,
    gv_ref,
):
    step = pl.program_id(0)
    block = s_ref.shape[1]
    head_dim = q_ref.shape[-1]
    half = head_dim // 2

    here = pl.ds(pl.multiple_of(step * block, block), block)
    queries = q_ref[here, :]
    grads = g_ref[0, here, :]
    kt_ref[step] = k_ref[here, :].T
    vt_ref[step] = v_ref[here, :].T
    gk_ref[step] = jnp.zeros(gk_ref.shape[1:], jnp.float32)
    gv_ref[step] = jnp.zeros(gv_ref.shape[1:], jnp.float32)

    def rows(tile):
        return pl.ds(pl.multiple_of(tile * block, block), block)

    scores = product(k_ref[here, :], queries, 1, 1)
    key_pos = lax.broadcasted_iota(jnp.int32, scores.shape, 0)
    query_pos = lax.broadcasted_iota(jnp.int32, scores.shape, 1)
    scores = jnp.where(key_pos <= query_pos, scores, -jnp.inf)
    s_ref[step] = scores

    def score(tile, top):
        scores = product(k_ref[rows(tile), :], queries, 1, 1)
        s_ref[tile] = scores
        return jnp.maximum(top, folded(scores, jnp.max))

    top = lax.fori_loop(0, step, score, folded(scores, jnp.max))
    factor = scale * math.log2(math.e)
    top = jnp.max(top, 0, keepdims=True) * factor

    def weigh(tile, sums):
        total, inner = sums
        weights = jnp.exp2(s_ref[tile] * factor - top)
        grad_probs = product(v_ref[rows(tile), :], grads, 1, 1)
        p_ref[tile] = weights
        d_ref[tile] = grad_probs
        return total + folded(weights, jnp.sum), inner + folded(weights * grad_probs, jnp.sum)

    zeros = jnp.zeros((8, block), jnp.float32)
    total, inner = lax.fori_loop(0, step + 1, weigh, (zeros, zeros))
    inverse = 1.0 / jnp.sum(total, 0, keepdims=True)
    inner = jnp.sum(inner, 0, keepdims=True) * inverse

    def back(tile, sums):
        att, grad_q = sums
        probs = p_ref[tile] * inverse
        probs_b = probs.astype(jnp.bfloat16)
        grad_scores = (probs * (d_ref[tile] - inner)).astype(jnp.bfloat16)
        gv_ref[tile] += product(probs_b, grads)
        gk_ref[tile] += product(grad_scores, queries)
        return att + product(vt_ref[tile], probs_b), grad_q + product(kt_ref[tile], grad_scores)

    zeros = jnp.zeros((head_dim, block), jnp.float32)
    att, grad_q = lax.fori_loop(0, step + 1, back, (zeros, zeros))

    def unrotate(grad, where):
        cosine, sine = cos_ref[:, where], sin_ref[:, where]
        first, second = grad[:half], grad[half:]
        factor = scale * proj_scale
        return (
            ((first * cosine + second * sine) * factor).astype(jnp.bfloat16),
            ((second * cosine - first * sine) * factor).astype(jnp.bfloat16),
        )

    att_ref[:, here] = att.astype(jnp.bfloat16)
    first, second = unrotate(grad_q, here)
    grad_ref[:half, here] = first
    grad_ref[half:head_dim, here] = second

    @pl.when(step == pl.num_programs(0) - 1)
    def finish():
        def keys(tile, carry):
            where = rows(tile)
            first, second = unrotate(gk_ref[tile].T, where)
            grad_ref[head_dim : head_dim + half, where] = first
            grad_ref[head_dim + half : 2 * head_dim, where] = second
            values = gv_ref[tile].T * proj_scale
            grad_ref[2 * head_dim :, where] = values.astype(jnp.bfloat16)
            return carry

        lax.fori_loop(0, pl.num_programs(0), keys, 0)


def attention(head, queries, keys, values, grads, cosine_t, sine_t, width):
    seq_len, head_dim = queries.shape
    block = min(BLOCK, seq_len)
    tiles = seq_len // block
    of_head = pl.BlockSpec((seq_len, head_dim), lambda i: (0, 0))
    stacked = pl.BlockSpec((1, seq_len, head_dim), lambda i: (head, 0, 0))
    whole = pl.BlockSpec((head_dim // 2, seq_len), lambda i: (0, 0))
    return pl.pallas_call(
        partial(attention_kernel, 1.0 / math.sqrt(head_dim), 1.0 / math.sqrt(width)),
        grid=(tiles,),
        in_specs=[of_head] * 3 + [stacked] + [whole] * 2,
        out_specs=[
            pl.BlockSpec((3 * head_dim, seq_len), lambda i: (0, 0)),
            pl.BlockSpec((head_dim, seq_len), lambda i: (0, 0)),
        ],
        out_shape=[
            jax.ShapeDtypeStruct((3 * head_dim, seq_len), jnp.bfloat16),
            jax.ShapeDtypeStruct((head_dim, seq_len), jnp.bfloat16),
        ],
        scratch_shapes=[pltpu.VMEM((tiles, block, block), jnp.float32)] * 3
        + [pltpu.VMEM((tiles, head_dim, block), jnp.bfloat16)] * 2
        + [pltpu.VMEM((tiles, block, head_dim), jnp.float32)] * 2,
        compiler_params=params(),
        cost_estimate=SHORT,
        name="attention",
    )(queries, keys, values, grads, cosine_t, sine_t)


def momenta_kernel(
    scale, grad_ref, att_ref, normed_ref, rows_ref, mqkv_ref, mout_ref, moved_ref
):
    three = grad_ref.shape[0]
    grad = product(grad_ref[...], normed_ref[...]).T.astype(jnp.bfloat16)
    moved = BETA * mqkv_ref[0].astype(jnp.float32) + grad.astype(jnp.float32)
    moved_ref[:, :three] = moved.astype(jnp.bfloat16)
    grad = (product(att_ref[...], rows_ref[...]) * scale).astype(jnp.bfloat16)
    moved = BETA * mout_ref[0].astype(jnp.float32) + grad.astype(jnp.float32)
    moved_ref[:, three:] = moved.T.astype(jnp.bfloat16)


def momenta(head, piece, grad_proj, attended, normed, rows, mom_qkv, mom_out, scale):
    first, count, block = piece
    seq_len = normed.shape[0]
    three, head_dim = grad_proj.shape[0], attended.shape[0]
    return pl.pallas_call(
        partial(momenta_kernel, scale),
        grid=(count,),
        in_specs=[
            pl.BlockSpec((three, seq_len), lambda i: (0, 0)),
            pl.BlockSpec((head_dim, seq_len), lambda i: (0, 0)),
            pl.BlockSpec((seq_len, block), lambda i: (0, first + i)),
            pl.BlockSpec((seq_len, block), lambda i: (0, first + i)),
            pl.BlockSpec((1, block, three), lambda i: (head, first + i, 0)),
            pl.BlockSpec((1, head_dim, block), lambda i: (head, 0, first + i)),
        ],
        out_specs=pl.BlockSpec((block, three + head_dim), lambda i: (i, 0)),
        out_shape=jax.ShapeDtypeStruct((count * block, three + head_dim), jnp.bfloat16),
        compiler_params=params(),
        cost_estimate=SHORT,
        name="momenta",
    )(grad_proj, attended, normed, rows, mom_qkv, mom_out)


def average_kernel(rate_ref, qkv, other_qkv, out, other_out, moment, other_moment, *refs):
    rate = rate_ref[0, 0]
    new_qkv, new_out, new_mom_qkv, new_mom_out = refs[-4:]
    three = qkv.shape[-1]

    def halfway(own, other):
        return ((own.astype(jnp.float32) + other.astype(jnp.float32)) * 0.5).astype(jnp.bfloat16)

    def moved(weight, moment):
        new = weight.astype(jnp.float32) - rate * moment.astype(jnp.float32)
        return new.astype(jnp.bfloat16)

    own, other = moment[:, :three], other_moment[:, :three]
    new_qkv[0, 0] = halfway(moved(qkv[0, 0], own), moved(other_qkv[0, 0], other))
    new_mom_qkv[0, 0] = halfway(own, other)
    own = moment[:, three:].astype(jnp.float32).T
    other = other_moment[:, three:].astype(jnp.float32).T
    new_out[0, 0] = halfway(moved(out[0, 0], own), moved(other_out[0, 0], other))
    new_mom_out[0, 0] = halfway(own, other)


def average(head, piece, rate, own, other, moment, other_moment, previous):
    first, count, block = piece
    (qkv, out), (other_qkv, other_out) = own, other
    three, head_dim = qkv.shape[-1], out.shape[2]
    high = pl.BlockSpec((1, 1, block, three), lambda i: (0, head, first + i, 0))
    wide = pl.BlockSpec((1, 1, head_dim, block), lambda i: (0, head, 0, first + i))
    packed = pl.BlockSpec((block, three + head_dim), lambda i: (i, 0))
    in_specs = [pl.BlockSpec(memory_space=pltpu.SMEM), high, high, wide, wide, packed, packed]
    args = [rate, qkv, other_qkv, out, other_out, moment, other_moment]
    aliases = {}
    if previous is not None:
        aliases = {len(args) + i: i for i in range(4)}
        args += list(previous)
        in_specs += [pl.BlockSpec(memory_space=pl.ANY)] * 4
    return pl.pallas_call(
        average_kernel,
        grid=(count,),
        in_specs=in_specs,
        out_specs=[high, wide] * 2,
        out_shape=[jax.ShapeDtypeStruct(w.shape, jnp.bfloat16) for w in own] * 2,
        input_output_aliases=aliases,
        compiler_params=params(),
        cost_estimate=SHORT,
        name="average",
    )(*args)


def pieces_of(head, heads, width):
    block = min(BLOCK, width)
    blocks = width // block
    if head < heads - 1 or blocks < 4:
        return [(0, blocks, block)]
    return [(0, blocks - 2, block), (blocks - 2, 1, block), (blocks - 1, 1, block)]


def update(by, inputs, out_grad, norm_gain, w_qkv, w_out, mom_qkv, mom_out, rate):
    own = (w_qkv, w_out)
    other = tuple(shifted(w, by) for w in own)
    w_qkv, w_out = w_qkv[0], w_out[0]

    rows_f = inputs.astype(jnp.float32)
    stats = lax.rsqrt(jnp.mean(rows_f * rows_f, -1, keepdims=True) + EPSILON)
    normed = (rows_f * stats * norm_gain[None, :]).astype(jnp.bfloat16)
    normed = lax.all_gather(normed, "fsdp", axis=0, tiled=True)
    rows = lax.all_gather(out_grad, "fsdp", axis=0, tiled=True)

    seq_len, width = normed.shape
    heads, head_dim, _ = w_out.shape
    out_scale = 1.0 / math.sqrt(HEADS * head_dim)
    cosine, sine = rotary_tables(seq_len, head_dim)
    full_cosine = jnp.concatenate([cosine, cosine], -1)
    full_sine = jnp.concatenate([-sine, sine], -1)
    grads = cotangent(rows, w_out, out_scale)
    made = []
    for head in range(heads):
        queries, keys, values = project(head, normed, w_qkv, full_cosine, full_sine)
        grad_proj, attended = attention(
            head, queries, keys, values, grads, cosine.T, sine.T, width
        )
        for piece in pieces_of(head, heads, width):
            moment = momenta(
                head, piece, grad_proj, attended, normed, rows, mom_qkv, mom_out, out_scale
            )
            normed, moment = lax.optimization_barrier((normed, moment))
            made.append((head, piece, moment, shifted(moment, by)))
    results = None
    for head, piece, moment, other_moment in made:
        results = average(head, piece, rate, own, other, moment, other_moment, results)
    return tuple(results)


def per_device(inputs, out_grad, norm_gain, w_qkv, w_out, mom_qkv, mom_out, step_index):
    rate = RATE * (step_index[0].astype(jnp.float32) + 1.0) / (4.0 * LEVELS)
    exponent = jnp.remainder(step_index[0], LEVELS)
    return lax.switch(
        exponent,
        [partial(update, 1 << level) for level in range(LEVELS)],
        inputs[0],
        out_grad[0],
        norm_gain[0],
        w_qkv,
        w_out,
        mom_qkv[0],
        mom_out[0],
        rate.reshape(1, 1),
    )


def solution(mesh):
    return jax.shard_map(
        per_device,
        mesh=mesh,
        in_specs=(
            P("gossip", "fsdp", None),
            P("gossip", "fsdp", None),
            P("gossip", None),
            P("gossip", "fsdp", None, None),
            P("gossip", "fsdp", None, None),
            P("gossip", "fsdp", None, None),
            P("gossip", "fsdp", None, None),
            P(),
        ),
        out_specs=(
            P("gossip", "fsdp", None, None),
            P("gossip", "fsdp", None, None),
            P("gossip", "fsdp", None, None),
            P("gossip", "fsdp", None, None),
        ),
        check_vma=False,
    )
```

```python
from functools import partial
import math

import jax
import jax.numpy as jnp
from jax import lax
from jax.experimental import pallas as pl
from jax.experimental.pallas import tpu as pltpu
from jax.sharding import PartitionSpec as P

HEADS = 16
LEVELS = 3

BETA = 0.9
RATE = 0.1
EPSILON = 1e-05

VMEM_LIMIT = 63 * 1024 * 1024
BLOCK = 512
CHUNK = 256
TILE = 512

SHORT = pl.CostEstimate(flops=1, bytes_accessed=1, transcendentals=0)


def product(left, right, left_dim=1, right_dim=0):
    return lax.dot_general(
        left, right, (((left_dim,), (right_dim,)), ((), ())), preferred_element_type=jnp.float32
    )


def in_chunks(size, chunk, body):
    chunk = min(chunk, size)

    def step(index, carry):
        body(pl.ds(pl.multiple_of(index * chunk, chunk), chunk))
        return carry

    lax.fori_loop(0, size // chunk, step, 0)


def params():
    return pltpu.CompilerParams(vmem_limit_bytes=VMEM_LIMIT)


def shifted(value, by):
    size = lax.axis_size("gossip")
    return lax.ppermute(value, "gossip", [(i, (i + by) % size) for i in range(size)])


def assemble_kernel(offsets, *refs):
    blocks, (out_ref, held, came, left) = refs[:-4], refs[-4:]
    me = lax.axis_index("fsdp")
    high = blocks[0].shape[0]
    inward, outward = [], []
    for number, (offset, block) in enumerate(zip(offsets, blocks)):
        place = pl.ds(pl.multiple_of((me ^ offset) * high, high), high)
        inward.append(pltpu.make_async_copy(block, held.at[number], came.at[number]))
        outward.append(
            pltpu.make_async_copy(held.at[number], out_ref.at[place, :], left.at[number])
        )
        inward[-1].start()
    for first, second in zip(inward, outward):
        first.wait()
        second.start()
    for copy in outward:
        copy.wait()


def gathered(rows):
    size = lax.axis_size("fsdp")
    blocks, offsets, bit = [rows], [0], size // 2
    while bit:
        pairs = [(i, i ^ bit) for i in range(size)]
        blocks += [lax.ppermute(block, "fsdp", pairs) for block in blocks]
        offsets += [offset ^ bit for offset in offsets]
        bit //= 2
    high, wide = rows.shape
    return pl.pallas_call(
        partial(assemble_kernel, offsets),
        in_specs=[pl.BlockSpec(memory_space=pl.ANY)] * size,
        out_specs=pl.BlockSpec(memory_space=pl.ANY),
        out_shape=jax.ShapeDtypeStruct((size * high, wide), rows.dtype),
        scratch_shapes=[
            pltpu.VMEM((size, high, wide), rows.dtype),
            pltpu.SemaphoreType.DMA((size,)),
            pltpu.SemaphoreType.DMA((size,)),
        ],
        compiler_params=params(),
        cost_estimate=SHORT,
        name="assemble",
    )(*blocks)


def rotary_tables(seq_len, head_dim):
    half = head_dim // 2
    frequency = jnp.exp(
        -math.log(10000.0) * 2.0 * jnp.arange(half, dtype=jnp.float32) / head_dim
    )
    angles = jnp.arange(seq_len).astype(jnp.float32)[:, None] * frequency[None, :]
    return jnp.cos(angles), jnp.sin(angles)


def project_kernel(scale, rows_ref, weight_ref, cos_ref, sin_ref, q_ref, k_ref, v_ref):
    width = cos_ref.shape[-1]

    def chunk(here):
        cosine, sine = cos_ref[here, :], sin_ref[here, :]
        projected = product(rows_ref[here, :], weight_ref[0]) * scale
        for which, out_ref in enumerate((q_ref, k_ref)):
            part = projected[:, which * width : (which + 1) * width]
            turned = part * cosine + pltpu.roll(part, width // 2, 1) * sine
            out_ref[here, :] = turned.astype(jnp.bfloat16)
        v_ref[here, :] = projected[:, 2 * width :].astype(jnp.bfloat16)

    in_chunks(rows_ref.shape[0], CHUNK, chunk)


def project(head, rows, weights, cosine, sine):
    seq_len, width = rows.shape
    three = weights.shape[-1]
    head_dim = three // 3
    block = min(BLOCK, seq_len)
    out = jax.ShapeDtypeStruct((seq_len, head_dim), jnp.bfloat16)
    out_spec = pl.BlockSpec((block, head_dim), lambda i: (i, 0))
    return pl.pallas_call(
        partial(project_kernel, 1.0 / math.sqrt(width)),
        grid=(seq_len // block,),
        in_specs=[
            pl.BlockSpec((block, width), lambda i: (i, 0)),
            pl.BlockSpec((1, width, three), lambda i: (head, 0, 0)),
            out_spec,
            out_spec,
        ],
        out_specs=[out_spec] * 3,
        out_shape=[out] * 3,
        compiler_params=params(),
        cost_estimate=SHORT,
        name="project",
    )(rows, weights, cosine, sine)


def cotangent_kernel(scale, rows_ref, weight_ref, out_ref):
    def of_head(head, carry):
        grads = product(rows_ref[...], weight_ref[head], 1, 1) * scale
        out_ref[head] = grads.astype(jnp.bfloat16)
        return carry

    lax.fori_loop(0, weight_ref.shape[0], of_head, 0)


def cotangent(rows, weights, scale):
    seq_len, width = rows.shape
    heads, head_dim, _ = weights.shape
    block = min(BLOCK, seq_len)
    return pl.pallas_call(
        partial(cotangent_kernel, scale),
        grid=(seq_len // block,),
        in_specs=[
            pl.BlockSpec((block, width), lambda i: (i, 0)),
            pl.BlockSpec((heads, head_dim, width), lambda i: (0, 0, 0)),
        ],
        out_specs=pl.BlockSpec((heads, block, head_dim), lambda i: (0, i, 0)),
        out_shape=jax.ShapeDtypeStruct((heads, seq_len, head_dim), jnp.bfloat16),
        compiler_params=params(),
        cost_estimate=SHORT,
        name="cotangent",
    )(rows, weights)


def folded(values, combine):
    rows, columns = values.shape
    return combine(values.reshape(rows // 8, 8, columns), 0)


def attention_kernel(
    scale,
    proj_scale,
    q_ref,
    k_ref,
    v_ref,
    g_ref,
    cos_ref,
    sin_ref,
    grad_ref,
    att_ref,
    s_ref,
    p_ref,
    d_ref,
    kt_ref,
    vt_ref,
    gk_ref,
    gv_ref,
):
    step = pl.program_id(0)
    _, tile_len, block = s_ref.shape
    head_dim = q_ref.shape[-1]
    half = head_dim // 2
    in_block = block // tile_len

    def rows(tile):
        return pl.ds(pl.multiple_of(tile * tile_len, tile_len), tile_len)

    here = pl.ds(pl.multiple_of(step * block, block), block)
    queries = q_ref[here, :]
    grads = g_ref[0, here, :]
    first_tile, tiles = step * in_block, (step + 1) * in_block

    def enter(tile, carry):
        kt_ref[tile] = k_ref[rows(tile), :].T
        vt_ref[tile] = v_ref[rows(tile), :].T
        gk_ref[tile] = jnp.zeros(gk_ref.shape[1:], jnp.float32)
        gv_ref[tile] = jnp.zeros(gv_ref.shape[1:], jnp.float32)
        return carry

    lax.fori_loop(first_tile, tiles, enter, 0)

    behind = lax.broadcasted_iota(jnp.int32, (tile_len, block), 0) - lax.broadcasted_iota(
        jnp.int32, (tile_len, block), 1
    )

    def score(tile, top):
        scores = product(k_ref[rows(tile), :], queries, 1, 1)
        scores = jnp.where(behind <= step * block - tile * tile_len, scores, -jnp.inf)
        s_ref[tile] = scores
        return jnp.maximum(top, folded(scores, jnp.max))

    top = lax.fori_loop(0, tiles, score, jnp.full((8, block), -jnp.inf, jnp.float32))
    factor = scale * math.log2(math.e)
    top = jnp.max(top, 0, keepdims=True) * factor

    def weigh(tile, sums):
        total, inner = sums
        weights = jnp.exp2(s_ref[tile] * factor - top)
        grad_probs = product(v_ref[rows(tile), :], grads, 1, 1)
        p_ref[tile] = weights
        d_ref[tile] = grad_probs
        return total + folded(weights, jnp.sum), inner + folded(weights * grad_probs, jnp.sum)

    zeros = jnp.zeros((8, block), jnp.float32)
    total, inner = lax.fori_loop(0, tiles, weigh, (zeros, zeros))
    inverse = 1.0 / jnp.sum(total, 0, keepdims=True)
    inner = jnp.sum(inner, 0, keepdims=True) * inverse

    def back(tile, sums):
        att, grad_q = sums
        probs = p_ref[tile] * inverse
        probs_b = probs.astype(jnp.bfloat16)
        grad_scores = (probs * (d_ref[tile] - inner)).astype(jnp.bfloat16)
        gv_ref[tile] += product(probs_b, grads)
        gk_ref[tile] += product(grad_scores, queries)
        return att + product(vt_ref[tile], probs_b), grad_q + product(kt_ref[tile], grad_scores)

    zeros = jnp.zeros((head_dim, block), jnp.float32)
    att, grad_q = lax.fori_loop(0, tiles, back, (zeros, zeros))

    def unrotate(grad, where):
        cosine, sine = cos_ref[:, where], sin_ref[:, where]
        first, second = grad[:half], grad[half:]
        factor = scale * proj_scale
        return (
            ((first * cosine + second * sine) * factor).astype(jnp.bfloat16),
            ((second * cosine - first * sine) * factor).astype(jnp.bfloat16),
        )

    att_ref[:, here] = att.astype(jnp.bfloat16)
    first, second = unrotate(grad_q, here)
    grad_ref[:half, here] = first
    grad_ref[half:head_dim, here] = second

    @pl.when(step == pl.num_programs(0) - 1)
    def finish():
        def keys(tile, carry):
            where = rows(tile)
            first, second = unrotate(gk_ref[tile].T, where)
            grad_ref[head_dim : head_dim + half, where] = first
            grad_ref[head_dim + half : 2 * head_dim, where] = second
            values = gv_ref[tile].T * proj_scale
            grad_ref[2 * head_dim :, where] = values.astype(jnp.bfloat16)
            return carry

        lax.fori_loop(0, tiles, keys, 0)


def attention(head, queries, keys, values, grads, cosine_t, sine_t, width):
    seq_len, head_dim = queries.shape
    block = min(BLOCK, seq_len)
    tile_len = min(TILE, block)
    tiles = seq_len // tile_len
    of_head = pl.BlockSpec((seq_len, head_dim), lambda i: (0, 0))
    stacked = pl.BlockSpec((1, seq_len, head_dim), lambda i: (head, 0, 0))
    whole = pl.BlockSpec((head_dim // 2, seq_len), lambda i: (0, 0))
    return pl.pallas_call(
        partial(attention_kernel, 1.0 / math.sqrt(head_dim), 1.0 / math.sqrt(width)),
        grid=(seq_len // block,),
        in_specs=[of_head] * 3 + [stacked] + [whole] * 2,
        out_specs=[
            pl.BlockSpec((3 * head_dim, seq_len), lambda i: (0, 0)),
            pl.BlockSpec((head_dim, seq_len), lambda i: (0, 0)),
        ],
        out_shape=[
            jax.ShapeDtypeStruct((3 * head_dim, seq_len), jnp.bfloat16),
            jax.ShapeDtypeStruct((head_dim, seq_len), jnp.bfloat16),
        ],
        scratch_shapes=[pltpu.VMEM((tiles, tile_len, block), jnp.float32)] * 3
        + [pltpu.VMEM((tiles, head_dim, tile_len), jnp.bfloat16)] * 2
        + [pltpu.VMEM((tiles, tile_len, head_dim), jnp.float32)] * 2,
        compiler_params=params(),
        cost_estimate=SHORT,
        name="attention",
    )(queries, keys, values, grads, cosine_t, sine_t)


def momenta_kernel(
    scale, grad_ref, att_ref, normed_ref, rows_ref, mqkv_ref, mout_ref, moved_ref
):
    three = grad_ref.shape[0]

    def chunk(here):
        grad = product(grad_ref[...], normed_ref[:, here]).T.astype(jnp.bfloat16)
        moved = BETA * mqkv_ref[0, here, :].astype(jnp.float32) + grad.astype(jnp.float32)
        moved_ref[here, :three] = moved.astype(jnp.bfloat16)
        grad = (product(att_ref[...], rows_ref[:, here]) * scale).astype(jnp.bfloat16)
        moved = BETA * mout_ref[0, :, here].astype(jnp.float32) + grad.astype(jnp.float32)
        moved_ref[here, three:] = moved.T.astype(jnp.bfloat16)

    in_chunks(moved_ref.shape[0], CHUNK, chunk)


def momenta(head, piece, grad_proj, attended, normed, rows, mom_qkv, mom_out, scale):
    first, count, block = piece
    seq_len = normed.shape[0]
    three, head_dim = grad_proj.shape[0], attended.shape[0]
    return pl.pallas_call(
        partial(momenta_kernel, scale),
        grid=(count,),
        in_specs=[
            pl.BlockSpec((three, seq_len), lambda i: (0, 0)),
            pl.BlockSpec((head_dim, seq_len), lambda i: (0, 0)),
            pl.BlockSpec((seq_len, block), lambda i: (0, first + i)),
            pl.BlockSpec((seq_len, block), lambda i: (0, first + i)),
            pl.BlockSpec((1, block, three), lambda i: (head, first + i, 0)),
            pl.BlockSpec((1, head_dim, block), lambda i: (head, 0, first + i)),
        ],
        out_specs=pl.BlockSpec((block, three + head_dim), lambda i: (i, 0)),
        out_shape=jax.ShapeDtypeStruct((count * block, three + head_dim), jnp.bfloat16),
        compiler_params=params(),
        cost_estimate=SHORT,
        name="momenta",
    )(grad_proj, attended, normed, rows, mom_qkv, mom_out)


def average_kernel(rate_ref, qkv, other_qkv, out, other_out, moment, other_moment, *refs):
    rate = rate_ref[0, 0]
    new_qkv, new_out, new_mom_qkv, new_mom_out = refs[-4:]
    three = qkv.shape[-1]

    def halfway(own, other):
        return ((own.astype(jnp.float32) + other.astype(jnp.float32)) * 0.5).astype(jnp.bfloat16)

    def moved(weight, moment):
        new = weight.astype(jnp.float32) - rate * moment.astype(jnp.float32)
        return new.astype(jnp.bfloat16)

    def chunk(here):
        own, other = moment[here, :three], other_moment[here, :three]
        new = halfway(moved(qkv[0, 0, here, :], own), moved(other_qkv[0, 0, here, :], other))
        new_qkv[0, 0, here, :] = new
        new_mom_qkv[0, 0, here, :] = halfway(own, other)
        own = moment[here, three:].astype(jnp.float32).T
        other = other_moment[here, three:].astype(jnp.float32).T
        new = halfway(moved(out[0, 0, :, here], own), moved(other_out[0, 0, :, here], other))
        new_out[0, 0, :, here] = new
        new_mom_out[0, 0, :, here] = halfway(own, other)

    in_chunks(moment.shape[0], 128, chunk)


def average(head, piece, rate, own, other, moment, other_moment, previous):
    first, count, block = piece
    (qkv, out), (other_qkv, other_out) = own, other
    three, head_dim = qkv.shape[-1], out.shape[2]
    high = pl.BlockSpec((1, 1, block, three), lambda i: (0, head, first + i, 0))
    wide = pl.BlockSpec((1, 1, head_dim, block), lambda i: (0, head, 0, first + i))
    packed = pl.BlockSpec((block, three + head_dim), lambda i: (i, 0))
    in_specs = [pl.BlockSpec(memory_space=pltpu.SMEM), high, high, wide, wide, packed, packed]
    args = [rate, qkv, other_qkv, out, other_out, moment, other_moment]
    aliases = {}
    if previous is not None:
        aliases = {len(args) + i: i for i in range(4)}
        args += list(previous)
        in_specs += [pl.BlockSpec(memory_space=pl.ANY)] * 4
    return pl.pallas_call(
        average_kernel,
        grid=(count,),
        in_specs=in_specs,
        out_specs=[high, wide] * 2,
        out_shape=[jax.ShapeDtypeStruct(w.shape, jnp.bfloat16) for w in own] * 2,
        input_output_aliases=aliases,
        compiler_params=params(),
        cost_estimate=SHORT,
        name="average",
    )(*args)


def pieces_of(head, heads, width):
    block = min(BLOCK, width)
    blocks = width // block
    if head < heads - 1 or blocks < 4:
        return [(0, blocks, block)]
    return [(0, blocks - 2, block), (blocks - 2, 1, block), (blocks - 1, 1, block)]


def update(by, inputs, out_grad, norm_gain, w_qkv, w_out, mom_qkv, mom_out, rate):
    own = (w_qkv, w_out)
    other_qkv = shifted(w_qkv, by)

    rows_f = inputs.astype(jnp.float32)
    stats = lax.rsqrt(jnp.mean(rows_f * rows_f, -1, keepdims=True) + EPSILON)
    normed = (rows_f * stats * norm_gain[None, :]).astype(jnp.bfloat16)
    normed = gathered(normed)
    rows = gathered(out_grad)
    late_out, normed = lax.optimization_barrier((w_out, normed))
    other = (other_qkv, shifted(late_out, by))
    w_qkv, w_out = w_qkv[0], w_out[0]

    seq_len, width = normed.shape
    heads, head_dim, _ = w_out.shape
    out_scale = 1.0 / math.sqrt(HEADS * head_dim)
    cosine, sine = rotary_tables(seq_len, head_dim)
    full_cosine = jnp.concatenate([cosine, cosine], -1)
    full_sine = jnp.concatenate([-sine, sine], -1)
    grads = cotangent(rows, w_out, out_scale)
    made = []
    for head in range(heads):
        queries, keys, values = project(head, normed, w_qkv, full_cosine, full_sine)
        grad_proj, attended = attention(
            head, queries, keys, values, grads, cosine.T, sine.T, width
        )
        for piece in pieces_of(head, heads, width):
            moment = momenta(
                head, piece, grad_proj, attended, normed, rows, mom_qkv, mom_out, out_scale
            )
            normed, moment = lax.optimization_barrier((normed, moment))
            made.append((head, piece, moment, shifted(moment, by)))
    results = None
    for head, piece, moment, other_moment in made:
        results = average(head, piece, rate, own, other, moment, other_moment, results)
    return tuple(results)


def per_device(inputs, out_grad, norm_gain, w_qkv, w_out, mom_qkv, mom_out, step_index):
    rate = RATE * (step_index[0].astype(jnp.float32) + 1.0) / (4.0 * LEVELS)
    exponent = jnp.remainder(step_index[0], LEVELS)
    return lax.switch(
        exponent,
        [partial(update, 1 << level) for level in range(LEVELS)],
        inputs[0],
        out_grad[0],
        norm_gain[0],
        w_qkv,
        w_out,
        mom_qkv[0],
        mom_out[0],
        rate.reshape(1, 1),
    )


def solution(mesh):
    return jax.shard_map(
        per_device,
        mesh=mesh,
        in_specs=(
            P("gossip", "fsdp", None),
            P("gossip", "fsdp", None),
            P("gossip", None),
            P("gossip", "fsdp", None, None),
            P("gossip", "fsdp", None, None),
            P("gossip", "fsdp", None, None),
            P("gossip", "fsdp", None, None),
            P(),
        ),
        out_specs=(
            P("gossip", "fsdp", None, None),
            P("gossip", "fsdp", None, None),
            P("gossip", "fsdp", None, None),
            P("gossip", "fsdp", None, None),
        ),
        check_vma=False,
    )
```

```python
from functools import partial
import math

import jax
import jax.numpy as jnp
from jax import lax
from jax.experimental import pallas as pl
from jax.experimental.pallas import tpu as pltpu
from jax.sharding import PartitionSpec as P

HEADS = 16
LEVELS = 3

BETA = 0.9
RATE = 0.1
EPSILON = 1e-05

VMEM_LIMIT = 63 * 1024 * 1024
BLOCK = 512
CHUNK = 256
TILE = 512

SHORT = pl.CostEstimate(flops=1, bytes_accessed=1, transcendentals=0)


def product(left, right, left_dim=1, right_dim=0):
    return lax.dot_general(
        left, right, (((left_dim,), (right_dim,)), ((), ())), preferred_element_type=jnp.float32
    )


def in_chunks(size, chunk, body):
    chunk = min(chunk, size)

    def step(index, carry):
        body(pl.ds(pl.multiple_of(index * chunk, chunk), chunk))
        return carry

    lax.fori_loop(0, size // chunk, step, 0)


def params():
    return pltpu.CompilerParams(vmem_limit_bytes=VMEM_LIMIT)


def shifted(value, by):
    size = lax.axis_size("gossip")
    return lax.ppermute(value, "gossip", [(i, (i + by) % size) for i in range(size)])


def exchanged(blocks, stage):
    size = lax.axis_size("fsdp")
    bit = size >> (stage + 1)
    pairs = [(i, i ^ bit) for i in range(size)]
    return blocks + [lax.ppermute(block, "fsdp", pairs) for block in blocks]


def offsets_of(size):
    offsets, bit = [0], size // 2
    while bit:
        offsets += [offset ^ bit for offset in offsets]
        bit //= 2
    return offsets


def assemble_kernel(offsets, *refs):
    blocks, (out_ref, held, came, left) = refs[:-4], refs[-4:]
    me = lax.axis_index("fsdp")
    high = blocks[0].shape[0]
    inward, outward = [], []
    for number, (offset, block) in enumerate(zip(offsets, blocks)):
        place = pl.ds(pl.multiple_of((me ^ offset) * high, high), high)
        inward.append(pltpu.make_async_copy(block, held.at[number], came.at[number]))
        outward.append(
            pltpu.make_async_copy(held.at[number], out_ref.at[place, :], left.at[number])
        )
        inward[-1].start()
    for first, second in zip(inward, outward):
        first.wait()
        second.start()
    for copy in outward:
        copy.wait()


def assembled(blocks):
    size = len(blocks)
    high, wide = blocks[0].shape
    return pl.pallas_call(
        partial(assemble_kernel, offsets_of(size)),
        in_specs=[pl.BlockSpec(memory_space=pl.ANY)] * size,
        out_specs=pl.BlockSpec(memory_space=pl.ANY),
        out_shape=jax.ShapeDtypeStruct((size * high, wide), blocks[0].dtype),
        scratch_shapes=[
            pltpu.VMEM((size, high, wide), blocks[0].dtype),
            pltpu.SemaphoreType.DMA((size,)),
            pltpu.SemaphoreType.DMA((size,)),
        ],
        compiler_params=params(),
        cost_estimate=SHORT,
        name="assemble",
    )(*blocks)


def rotary_tables(seq_len, head_dim):
    half = head_dim // 2
    column = jnp.arange(head_dim)
    frequency = jnp.exp(
        -math.log(10000.0) * 2.0 * (column % half).astype(jnp.float32) / head_dim
    )
    angles = jnp.arange(seq_len).astype(jnp.float32)[:, None] * frequency[None, :]
    sign = jnp.where(column < half, -1.0, 1.0)
    return jnp.cos(angles), jnp.sin(angles) * sign[None, :]


def norm_kernel(rows_ref, gain_ref, out_ref):
    def chunk(here):
        rows = rows_ref[here, :].astype(jnp.float32)
        stats = lax.rsqrt(jnp.mean(rows * rows, -1, keepdims=True) + EPSILON)
        out_ref[here, :] = (rows * stats * gain_ref[...]).astype(jnp.bfloat16)

    in_chunks(rows_ref.shape[0], 64, chunk)


def normalised(rows, gain):
    high, wide = rows.shape
    block = min(256, high)
    of_rows = pl.BlockSpec((block, wide), lambda i: (i, 0))
    return pl.pallas_call(
        norm_kernel,
        grid=(high // block,),
        in_specs=[of_rows, pl.BlockSpec((1, wide), lambda i: (0, 0))],
        out_specs=of_rows,
        out_shape=jax.ShapeDtypeStruct(rows.shape, jnp.bfloat16),
        compiler_params=params(),
        cost_estimate=SHORT,
        name="normalised",
    )(rows, gain)


def project_kernel(scale, rows_ref, weight_ref, cos_ref, sin_ref, q_ref, k_ref, v_ref):
    width = cos_ref.shape[-1]

    def of_head(head, carry):
        def chunk(here):
            cosine, sine = cos_ref[here, :], sin_ref[here, :]
            projected = product(rows_ref[here, :], weight_ref[head]) * scale
            for which, out_ref in enumerate((q_ref, k_ref)):
                part = projected[:, which * width : (which + 1) * width]
                turned = part * cosine + pltpu.roll(part, width // 2, 1) * sine
                out_ref[head, here, :] = turned.astype(jnp.bfloat16)
            v_ref[head, here, :] = projected[:, 2 * width :].astype(jnp.bfloat16)

        in_chunks(rows_ref.shape[0], CHUNK, chunk)
        return carry

    lax.fori_loop(0, weight_ref.shape[0], of_head, 0)


def project(rows, weights, cosine, sine):
    seq_len, width = rows.shape
    heads, _, three = weights.shape
    head_dim = three // 3
    block = min(BLOCK, seq_len)
    table = pl.BlockSpec((block, head_dim), lambda i: (i, 0))
    return pl.pallas_call(
        partial(project_kernel, 1.0 / math.sqrt(width)),
        grid=(seq_len // block,),
        in_specs=[
            pl.BlockSpec((block, width), lambda i: (i, 0)),
            pl.BlockSpec((heads, width, three), lambda i: (0, 0, 0)),
            table,
            table,
        ],
        out_specs=[pl.BlockSpec((heads, block, head_dim), lambda i: (0, i, 0))] * 3,
        out_shape=[jax.ShapeDtypeStruct((heads, seq_len, head_dim), jnp.bfloat16)] * 3,
        compiler_params=params(),
        cost_estimate=SHORT,
        name="project",
    )(rows, weights, cosine, sine)


def cotangent_kernel(scale, rows_ref, weight_ref, out_ref):
    heads, head_dim, width = weight_ref.shape
    some = math.gcd(heads, 2)

    def of_heads(index, carry):
        first = index * some
        weights = weight_ref[pl.ds(first, some)].reshape(some * head_dim, width)
        grads = (product(rows_ref[...], weights, 1, 1) * scale).astype(jnp.bfloat16)
        for number in range(some):
            out_ref[first + number] = grads[:, number * head_dim : (number + 1) * head_dim]
        return carry

    lax.fori_loop(0, heads // some, of_heads, 0)


def cotangent(rows, weights, scale):
    seq_len, width = rows.shape
    heads, head_dim, _ = weights.shape
    block = min(BLOCK, seq_len)
    return pl.pallas_call(
        partial(cotangent_kernel, scale),
        grid=(seq_len // block,),
        in_specs=[
            pl.BlockSpec((block, width), lambda i: (i, 0)),
            pl.BlockSpec((heads, head_dim, width), lambda i: (0, 0, 0)),
        ],
        out_specs=pl.BlockSpec((heads, block, head_dim), lambda i: (0, i, 0)),
        out_shape=jax.ShapeDtypeStruct((heads, seq_len, head_dim), jnp.bfloat16),
        compiler_params=params(),
        cost_estimate=SHORT,
        name="cotangent",
    )(rows, weights)


def folded(values, combine):
    rows, columns = values.shape
    return combine(values.reshape(rows // 8, 8, columns), 0)


def attention_kernel(
    scale,
    proj_scale,
    q_ref,
    k_ref,
    v_ref,
    g_ref,
    cos_ref,
    sin_ref,
    grad_ref,
    att_ref,
    s_ref,
    p_ref,
    d_ref,
    kt_ref,
    vt_ref,
    gk_ref,
    gv_ref,
):
    step = pl.program_id(1)
    _, tile_len, block = s_ref.shape
    head_dim = q_ref.shape[-1]
    half = head_dim // 2
    in_block = block // tile_len

    def rows(tile):
        return pl.ds(pl.multiple_of(tile * tile_len, tile_len), tile_len)

    here = pl.ds(pl.multiple_of(step * block, block), block)
    queries = q_ref[0, here, :]
    grads = g_ref[0, here, :]
    first_tile, tiles = step * in_block, (step + 1) * in_block

    def enter(tile, carry):
        kt_ref[tile] = k_ref[0, rows(tile), :].T
        vt_ref[tile] = v_ref[0, rows(tile), :].T
        gk_ref[tile] = jnp.zeros(gk_ref.shape[1:], jnp.float32)
        gv_ref[tile] = jnp.zeros(gv_ref.shape[1:], jnp.float32)
        return carry

    lax.fori_loop(first_tile, tiles, enter, 0)

    behind = lax.broadcasted_iota(jnp.int32, (tile_len, block), 0) - lax.broadcasted_iota(
        jnp.int32, (tile_len, block), 1
    )

    def score(tile, top):
        scores = product(k_ref[0, rows(tile), :], queries, 1, 1)
        scores = jnp.where(behind <= step * block - tile * tile_len, scores, -jnp.inf)
        s_ref[tile] = scores
        return jnp.maximum(top, folded(scores, jnp.max))

    top = lax.fori_loop(0, tiles, score, jnp.full((8, block), -jnp.inf, jnp.float32))
    factor = scale * math.log2(math.e)
    top = jnp.max(top, 0, keepdims=True) * factor

    def weigh(tile, sums):
        total, inner = sums
        weights = jnp.exp2(s_ref[tile] * factor - top)
        grad_probs = product(v_ref[0, rows(tile), :], grads, 1, 1)
        p_ref[tile] = weights
        d_ref[tile] = grad_probs
        return total + folded(weights, jnp.sum), inner + folded(weights * grad_probs, jnp.sum)

    zeros = jnp.zeros((8, block), jnp.float32)
    total, inner = lax.fori_loop(0, tiles, weigh, (zeros, zeros))
    inverse = 1.0 / jnp.sum(total, 0, keepdims=True)
    inner = jnp.sum(inner, 0, keepdims=True) * inverse

    def back(tile, sums):
        att, grad_q = sums
        probs = p_ref[tile] * inverse
        probs_b = probs.astype(jnp.bfloat16)
        grad_scores = (probs * (d_ref[tile] - inner)).astype(jnp.bfloat16)
        gv_ref[tile] += product(probs_b, grads)
        gk_ref[tile] += product(grad_scores, queries)
        return att + product(vt_ref[tile], probs_b), grad_q + product(kt_ref[tile], grad_scores)

    zeros = jnp.zeros((head_dim, block), jnp.float32)
    att, grad_q = lax.fori_loop(0, tiles, back, (zeros, zeros))

    att_ref[0, :, here] = att.astype(jnp.bfloat16)
    cosine, sine = cos_ref[here, :].T, sin_ref[here, :].T
    turned = grad_q * cosine - pltpu.roll(grad_q, half, 0) * sine
    grad_ref[0, :head_dim, here] = (turned * (scale * proj_scale)).astype(jnp.bfloat16)

    @pl.when(step == pl.num_programs(1) - 1)
    def finish():
        def keys(tile, carry):
            where = rows(tile)
            grad_k = gk_ref[tile]
            turned = grad_k * cos_ref[where, :] - pltpu.roll(grad_k, half, 1) * sin_ref[where, :]
            turned = (turned * (scale * proj_scale)).T
            grad_ref[0, head_dim : 2 * head_dim, where] = turned.astype(jnp.bfloat16)
            values = gv_ref[tile].T * proj_scale
            grad_ref[0, 2 * head_dim :, where] = values.astype(jnp.bfloat16)
            return carry

        lax.fori_loop(0, tiles, keys, 0)


def attention(group, queries, keys, values, grads, cosine, sine, width):
    first, count = group
    _, seq_len, head_dim = queries.shape
    block = min(BLOCK, seq_len)
    tile_len = min(TILE, block)
    tiles = seq_len // tile_len
    of_head = pl.BlockSpec((1, seq_len, head_dim), lambda h, i: (first + h, 0, 0))
    table = pl.BlockSpec((seq_len, head_dim), lambda h, i: (0, 0))
    return pl.pallas_call(
        partial(attention_kernel, 1.0 / math.sqrt(head_dim), 1.0 / math.sqrt(width)),
        grid=(count, seq_len // block),
        in_specs=[of_head] * 4 + [table] * 2,
        out_specs=[
            pl.BlockSpec((1, 3 * head_dim, seq_len), lambda h, i: (h, 0, 0)),
            pl.BlockSpec((1, head_dim, seq_len), lambda h, i: (h, 0, 0)),
        ],
        out_shape=[
            jax.ShapeDtypeStruct((count, 3 * head_dim, seq_len), jnp.bfloat16),
            jax.ShapeDtypeStruct((count, head_dim, seq_len), jnp.bfloat16),
        ],
        scratch_shapes=[pltpu.VMEM((tiles, tile_len, block), jnp.float32)] * 3
        + [pltpu.VMEM((tiles, head_dim, tile_len), jnp.bfloat16)] * 2
        + [pltpu.VMEM((tiles, tile_len, head_dim), jnp.float32)] * 2,
        compiler_params=params(),
        cost_estimate=SHORT,
        name="attention",
    )(queries, keys, values, grads, cosine, sine)


def momenta_kernel(
    scale, grad_ref, att_ref, normed_ref, rows_ref, mqkv_ref, mout_ref, moved_ref
):
    count, three, _ = grad_ref.shape

    def of_head(head, carry):
        def chunk(here):
            grad = product(grad_ref[head], normed_ref[:, here]).T.astype(jnp.bfloat16)
            moved = BETA * mqkv_ref[head, here, :].astype(jnp.float32) + grad.astype(jnp.float32)
            moved_ref[head, here, :three] = moved.astype(jnp.bfloat16)
            grad = (product(att_ref[head], rows_ref[:, here]) * scale).astype(jnp.bfloat16)
            moved = BETA * mout_ref[head, :, here].astype(jnp.float32) + grad.astype(jnp.float32)
            moved_ref[head, here, three:] = moved.T.astype(jnp.bfloat16)

        in_chunks(moved_ref.shape[1], CHUNK, chunk)
        return carry

    lax.fori_loop(0, count, of_head, 0)


def momenta(group, piece, grad_proj, attended, normed, rows, mom_qkv, mom_out, scale):
    first, count, block = piece
    start, heads = group
    seq_len = normed.shape[0]
    three, head_dim = grad_proj.shape[1], attended.shape[1]
    group_index = start // heads
    return pl.pallas_call(
        partial(momenta_kernel, scale),
        grid=(count,),
        in_specs=[
            pl.BlockSpec((heads, three, seq_len), lambda i: (0, 0, 0)),
            pl.BlockSpec((heads, head_dim, seq_len), lambda i: (0, 0, 0)),
            pl.BlockSpec((seq_len, block), lambda i: (0, first + i)),
            pl.BlockSpec((seq_len, block), lambda i: (0, first + i)),
            pl.BlockSpec((heads, block, three), lambda i: (group_index, first + i, 0)),
            pl.BlockSpec((heads, head_dim, block), lambda i: (group_index, 0, first + i)),
        ],
        out_specs=pl.BlockSpec((heads, block, three + head_dim), lambda i: (0, i, 0)),
        out_shape=jax.ShapeDtypeStruct((heads, count * block, three + head_dim), jnp.bfloat16),
        compiler_params=params(),
        cost_estimate=SHORT,
        name="momenta",
    )(grad_proj, attended, normed, rows, mom_qkv, mom_out)


def average_kernel(rate_ref, qkv, other_qkv, out, other_out, moment, other_moment, *refs):
    rate = rate_ref[0, 0]
    new_qkv, new_out, new_mom_qkv, new_mom_out = refs[-4:]
    three = qkv.shape[-1]

    def halfway(own, other):
        return ((own.astype(jnp.float32) + other.astype(jnp.float32)) * 0.5).astype(jnp.bfloat16)

    def moved(weight, moment):
        new = weight.astype(jnp.float32) - rate * moment.astype(jnp.float32)
        return new.astype(jnp.bfloat16)

    def chunk(here):
        own, other = moment[0, here, :three], other_moment[0, here, :three]
        new = halfway(moved(qkv[0, 0, here, :], own), moved(other_qkv[0, 0, here, :], other))
        new_qkv[0, 0, here, :] = new
        new_mom_qkv[0, 0, here, :] = halfway(own, other)
        own = moment[0, here, three:].astype(jnp.float32).T
        other = other_moment[0, here, three:].astype(jnp.float32).T
        new = halfway(moved(out[0, 0, :, here], own), moved(other_out[0, 0, :, here], other))
        new_out[0, 0, :, here] = new
        new_mom_out[0, 0, :, here] = halfway(own, other)

    in_chunks(moment.shape[1], 128, chunk)


def average(group, piece, rate, own, other, moment, other_moment, previous):
    first, count, block = piece
    start, heads = group
    (qkv, out), (other_qkv, other_out) = own, other
    three, head_dim = qkv.shape[-1], out.shape[2]
    high = pl.BlockSpec((1, 1, block, three), lambda h, i: (0, start + h, first + i, 0))
    wide = pl.BlockSpec((1, 1, head_dim, block), lambda h, i: (0, start + h, 0, first + i))
    packed = pl.BlockSpec((1, block, three + head_dim), lambda h, i: (h, i, 0))
    in_specs = [pl.BlockSpec(memory_space=pltpu.SMEM), high, high, wide, wide, packed, packed]
    args = [rate, qkv, other_qkv, out, other_out, moment, other_moment]
    aliases = {}
    if previous is not None:
        aliases = {len(args) + i: i for i in range(4)}
        args += list(previous)
        in_specs += [pl.BlockSpec(memory_space=pl.ANY)] * 4
    return pl.pallas_call(
        average_kernel,
        grid=(heads, count),
        in_specs=in_specs,
        out_specs=[high, wide] * 2,
        out_shape=[jax.ShapeDtypeStruct(w.shape, jnp.bfloat16) for w in own] * 2,
        input_output_aliases=aliases,
        compiler_params=params(),
        cost_estimate=SHORT,
        name="average",
    )(*args)


def pieces_of(last, width):
    if not last or width % BLOCK or width < 2 * BLOCK:
        block = min(BLOCK, width)
        return [(0, width // block, block)]
    return [(0, width // BLOCK - 1, BLOCK), (width // CHUNK - 2, 2, CHUNK)]


def update(by, inputs, out_grad, norm_gain, w_qkv, w_out, mom_qkv, mom_out, rate):
    own = (w_qkv, w_out)
    other_qkv = shifted(w_qkv, by)

    normed = normalised(inputs, norm_gain)
    blocks, row_blocks = exchanged([normed], 0), exchanged([out_grad], 0)
    stage = 1
    while len(blocks) < lax.axis_size("fsdp"):
        blocks = exchanged(blocks, stage)
        stage += 1
    normed = assembled(blocks)
    other_out = shifted(w_out, by)
    w_qkv, w_out = w_qkv[0], w_out[0]

    seq_len, width = normed.shape
    heads, head_dim, _ = w_out.shape
    out_scale = 1.0 / math.sqrt(HEADS * head_dim)
    tables = rotary_tables(seq_len, head_dim)
    parts = project(normed, w_qkv, *tables)
    row_blocks[-1], parts = lax.optimization_barrier((row_blocks[-1], parts))
    stage = 1
    while len(row_blocks) < lax.axis_size("fsdp"):
        row_blocks = exchanged(row_blocks, stage)
        stage += 1
    rows = assembled(row_blocks)
    grads = cotangent(rows, w_out, out_scale)

    made = []
    some = max(heads // 2, 1)
    for start in range(0, heads, some):
        group = (start, some)
        grad_proj, attended = attention(group, *parts, grads, *tables, width)
        if start == 0:
            grad_proj, other_qkv = lax.optimization_barrier((grad_proj, other_qkv))
        if start + some == heads:
            grad_proj, other_out = lax.optimization_barrier((grad_proj, other_out))
        for piece in pieces_of(start + some == heads, width):
            moment = momenta(
                group, piece, grad_proj, attended, normed, rows, mom_qkv, mom_out, out_scale
            )
            grads, normed, moment = lax.optimization_barrier((grads, normed, moment))
            made.append((group, piece, moment, shifted(moment, by)))
    results, other = None, (other_qkv, other_out)
    for group, piece, moment, other_moment in made:
        results = average(group, piece, rate, own, other, moment, other_moment, results)
    return tuple(results)


def per_device(inputs, out_grad, norm_gain, w_qkv, w_out, mom_qkv, mom_out, step_index):
    rate = RATE * (step_index[0].astype(jnp.float32) + 1.0) / (4.0 * LEVELS)
    exponent = jnp.remainder(step_index[0], LEVELS)
    return lax.switch(
        exponent,
        [partial(update, 1 << level) for level in range(LEVELS)],
        inputs[0],
        out_grad[0],
        norm_gain,
        w_qkv,
        w_out,
        mom_qkv[0],
        mom_out[0],
        rate.reshape(1, 1),
    )


def solution(mesh):
    return jax.shard_map(
        per_device,
        mesh=mesh,
        in_specs=(
            P("gossip", "fsdp", None),
            P("gossip", "fsdp", None),
            P("gossip", None),
            P("gossip", "fsdp", None, None),
            P("gossip", "fsdp", None, None),
            P("gossip", "fsdp", None, None),
            P("gossip", "fsdp", None, None),
            P(),
        ),
        out_specs=(
            P("gossip", "fsdp", None, None),
            P("gossip", "fsdp", None, None),
            P("gossip", "fsdp", None, None),
            P("gossip", "fsdp", None, None),
        ),
        check_vma=False,
    )
```

```python
from functools import partial
import math

import jax
import jax.numpy as jnp
from jax import lax
from jax.experimental import pallas as pl
from jax.experimental.pallas import tpu as pltpu
from jax.sharding import PartitionSpec as P

HEADS = 16
LEVELS = 3

BETA = 0.9
RATE = 0.1
EPSILON = 1e-05

VMEM_LIMIT = 63 * 1024 * 1024
BLOCK = 512
CHUNK = 256
TILE = 512
PARTS = 2

SHORT = pl.CostEstimate(flops=1, bytes_accessed=1, transcendentals=0)


def product(left, right, left_dim=1, right_dim=0):
    return lax.dot_general(
        left, right, (((left_dim,), (right_dim,)), ((), ())), preferred_element_type=jnp.float32
    )


def in_chunks(size, chunk, body):
    chunk = min(chunk, size)

    def step(index, carry):
        body(pl.ds(pl.multiple_of(index * chunk, chunk), chunk))
        return carry

    lax.fori_loop(0, size // chunk, step, 0)


def params():
    return pltpu.CompilerParams(vmem_limit_bytes=VMEM_LIMIT)


def shifted(value, by):
    size = lax.axis_size("gossip")
    return lax.ppermute(value, "gossip", [(i, (i + by) % size) for i in range(size)])


def exchanged(blocks, stage):
    size = lax.axis_size("fsdp")
    bit = size >> (stage + 1)
    pairs = [(i, i ^ bit) for i in range(size)]
    return blocks + [lax.ppermute(block, "fsdp", pairs) for block in blocks]


def places_of(size, parts):
    places, bit = [(0, part) for part in range(parts)], size // 2
    while bit:
        places += [(offset ^ bit, part) for offset, part in places]
        bit //= 2
    return places


def assemble_kernel(places, *refs):
    blocks, (out_ref, held, came, left) = refs[:-4], refs[-4:]
    me = lax.axis_index("fsdp")
    high = blocks[0].shape[0]
    inward, outward = [], []
    parts = 1 + max(part for _, part in places)
    for number, ((offset, part), block) in enumerate(zip(places, blocks)):
        place = pl.ds(pl.multiple_of(((me ^ offset) * parts + part) * high, high), high)
        inward.append(pltpu.make_async_copy(block, held.at[number], came.at[number]))
        outward.append(
            pltpu.make_async_copy(held.at[number], out_ref.at[place, :], left.at[number])
        )
        inward[-1].start()
    for first, second in zip(inward, outward):
        first.wait()
        second.start()
    for copy in outward:
        copy.wait()


def assembled(blocks):
    size, devices = len(blocks), lax.axis_size("fsdp")
    high, wide = blocks[0].shape
    return pl.pallas_call(
        partial(assemble_kernel, places_of(devices, size // devices)),
        in_specs=[pl.BlockSpec(memory_space=pl.ANY)] * size,
        out_specs=pl.BlockSpec(memory_space=pl.ANY),
        out_shape=jax.ShapeDtypeStruct((size * high, wide), blocks[0].dtype),
        scratch_shapes=[
            pltpu.VMEM((size, high, wide), blocks[0].dtype),
            pltpu.SemaphoreType.DMA((size,)),
            pltpu.SemaphoreType.DMA((size,)),
        ],
        compiler_params=params(),
        cost_estimate=SHORT,
        name="assemble",
    )(*blocks)


def rotary_tables(seq_len, head_dim):
    half = head_dim // 2
    column = jnp.arange(head_dim)
    frequency = jnp.exp(
        -math.log(10000.0) * 2.0 * (column % half).astype(jnp.float32) / head_dim
    )
    angles = jnp.arange(seq_len).astype(jnp.float32)[:, None] * frequency[None, :]
    sign = jnp.where(column < half, -1.0, 1.0)
    return jnp.cos(angles), jnp.sin(angles) * sign[None, :]


def norm_kernel(rows_ref, gain_ref, out_ref):
    def chunk(here):
        rows = rows_ref[here, :].astype(jnp.float32)
        stats = lax.rsqrt(jnp.mean(rows * rows, -1, keepdims=True) + EPSILON)
        out_ref[here, :] = (rows * stats * gain_ref[...]).astype(jnp.bfloat16)

    in_chunks(rows_ref.shape[0], 64, chunk)


def normalised(rows, gain, part):
    high, wide = rows.shape
    block = high // PARTS
    return pl.pallas_call(
        norm_kernel,
        grid=(1,),
        in_specs=[
            pl.BlockSpec((block, wide), lambda i: (part, 0)),
            pl.BlockSpec((1, wide), lambda i: (0, 0)),
        ],
        out_specs=pl.BlockSpec((block, wide), lambda i: (0, 0)),
        out_shape=jax.ShapeDtypeStruct((block, wide), jnp.bfloat16),
        compiler_params=params(),
        cost_estimate=SHORT,
        name="normalised",
    )(rows, gain)


def project_kernel(scale, rows_ref, weight_ref, cos_ref, sin_ref, q_ref, k_ref, v_ref):
    width = cos_ref.shape[-1]

    def of_head(head, carry):
        def chunk(here):
            cosine, sine = cos_ref[here, :], sin_ref[here, :]
            projected = product(rows_ref[here, :], weight_ref[head]) * scale
            for which, out_ref in enumerate((q_ref, k_ref)):
                part = projected[:, which * width : (which + 1) * width]
                turned = part * cosine + pltpu.roll(part, width // 2, 1) * sine
                out_ref[head, here, :] = turned.astype(jnp.bfloat16)
            v_ref[head, here, :] = projected[:, 2 * width :].astype(jnp.bfloat16)

        in_chunks(rows_ref.shape[0], CHUNK, chunk)
        return carry

    lax.fori_loop(0, weight_ref.shape[0], of_head, 0)


def project(rows, weights, cosine, sine):
    seq_len, width = rows.shape
    heads, _, three = weights.shape
    head_dim = three // 3
    block = min(BLOCK, seq_len)
    table = pl.BlockSpec((block, head_dim), lambda i: (i, 0))
    return pl.pallas_call(
        partial(project_kernel, 1.0 / math.sqrt(width)),
        grid=(seq_len // block,),
        in_specs=[
            pl.BlockSpec((block, width), lambda i: (i, 0)),
            pl.BlockSpec((heads, width, three), lambda i: (0, 0, 0)),
            table,
            table,
        ],
        out_specs=[pl.BlockSpec((heads, block, head_dim), lambda i: (0, i, 0))] * 3,
        out_shape=[jax.ShapeDtypeStruct((heads, seq_len, head_dim), jnp.bfloat16)] * 3,
        compiler_params=params(),
        cost_estimate=SHORT,
        name="project",
    )(rows, weights, cosine, sine)


def cotangent_kernel(scale, rows_ref, weight_ref, out_ref):
    heads, head_dim, width = weight_ref.shape
    some = math.gcd(heads, 2)

    def of_heads(index, carry):
        first = index * some
        weights = weight_ref[pl.ds(first, some)].reshape(some * head_dim, width)
        grads = (product(rows_ref[...], weights, 1, 1) * scale).astype(jnp.bfloat16)
        for number in range(some):
            out_ref[first + number] = grads[:, number * head_dim : (number + 1) * head_dim]
        return carry

    lax.fori_loop(0, heads // some, of_heads, 0)


def cotangent(rows, weights, scale):
    seq_len, width = rows.shape
    heads, head_dim, _ = weights.shape
    block = min(BLOCK, seq_len)
    return pl.pallas_call(
        partial(cotangent_kernel, scale),
        grid=(seq_len // block,),
        in_specs=[
            pl.BlockSpec((block, width), lambda i: (i, 0)),
            pl.BlockSpec((heads, head_dim, width), lambda i: (0, 0, 0)),
        ],
        out_specs=pl.BlockSpec((heads, block, head_dim), lambda i: (0, i, 0)),
        out_shape=jax.ShapeDtypeStruct((heads, seq_len, head_dim), jnp.bfloat16),
        compiler_params=params(),
        cost_estimate=SHORT,
        name="cotangent",
    )(rows, weights)


def folded(values, combine):
    rows, columns = values.shape
    return combine(values.reshape(rows // 8, 8, columns), 0)


def attention_kernel(
    scale,
    proj_scale,
    q_ref,
    k_ref,
    v_ref,
    g_ref,
    cos_ref,
    sin_ref,
    grad_ref,
    att_ref,
    s_ref,
    p_ref,
    d_ref,
    kt_ref,
    vt_ref,
    gk_ref,
    gv_ref,
):
    step = pl.program_id(1)
    _, tile_len, block = s_ref.shape
    head_dim = q_ref.shape[-1]
    half = head_dim // 2
    in_block = block // tile_len

    def rows(tile):
        return pl.ds(pl.multiple_of(tile * tile_len, tile_len), tile_len)

    here = pl.ds(pl.multiple_of(step * block, block), block)
    queries = q_ref[0, here, :]
    grads = g_ref[0, here, :]
    first_tile, tiles = step * in_block, (step + 1) * in_block

    def enter(tile, carry):
        kt_ref[tile] = k_ref[0, rows(tile), :].T
        vt_ref[tile] = v_ref[0, rows(tile), :].T
        gk_ref[tile] = jnp.zeros(gk_ref.shape[1:], jnp.float32)
        gv_ref[tile] = jnp.zeros(gv_ref.shape[1:], jnp.float32)
        return carry

    lax.fori_loop(first_tile, tiles, enter, 0)

    behind = lax.broadcasted_iota(jnp.int32, (tile_len, block), 0) - lax.broadcasted_iota(
        jnp.int32, (tile_len, block), 1
    )

    def score(tile, top):
        scores = product(k_ref[0, rows(tile), :], queries, 1, 1)
        scores = jnp.where(behind <= step * block - tile * tile_len, scores, -jnp.inf)
        s_ref[tile] = scores
        return jnp.maximum(top, folded(scores, jnp.max))

    top = lax.fori_loop(0, tiles, score, jnp.full((8, block), -jnp.inf, jnp.float32))
    factor = scale * math.log2(math.e)
    top = jnp.max(top, 0, keepdims=True) * factor

    def weigh(tile, sums):
        total, inner = sums
        weights = jnp.exp2(s_ref[tile] * factor - top)
        grad_probs = product(v_ref[0, rows(tile), :], grads, 1, 1)
        p_ref[tile] = weights
        d_ref[tile] = grad_probs
        return total + folded(weights, jnp.sum), inner + folded(weights * grad_probs, jnp.sum)

    zeros = jnp.zeros((8, block), jnp.float32)
    total, inner = lax.fori_loop(0, tiles, weigh, (zeros, zeros))
    inverse = 1.0 / jnp.sum(total, 0, keepdims=True)
    inner = jnp.sum(inner, 0, keepdims=True) * inverse

    def back(tile, sums):
        att, grad_q = sums
        probs = p_ref[tile] * inverse
        probs_b = probs.astype(jnp.bfloat16)
        grad_scores = (probs * (d_ref[tile] - inner)).astype(jnp.bfloat16)
        gv_ref[tile] += product(probs_b, grads)
        gk_ref[tile] += product(grad_scores, queries)
        return att + product(vt_ref[tile], probs_b), grad_q + product(kt_ref[tile], grad_scores)

    zeros = jnp.zeros((head_dim, block), jnp.float32)
    att, grad_q = lax.fori_loop(0, tiles, back, (zeros, zeros))

    att_ref[0, :, here] = att.astype(jnp.bfloat16)
    cosine, sine = cos_ref[here, :].T, sin_ref[here, :].T
    turned = grad_q * cosine - pltpu.roll(grad_q, half, 0) * sine
    grad_ref[0, :head_dim, here] = (turned * (scale * proj_scale)).astype(jnp.bfloat16)

    @pl.when(step == pl.num_programs(1) - 1)
    def finish():
        def keys(tile, carry):
            where = rows(tile)
            grad_k = gk_ref[tile]
            turned = grad_k * cos_ref[where, :] - pltpu.roll(grad_k, half, 1) * sin_ref[where, :]
            turned = (turned * (scale * proj_scale)).T
            grad_ref[0, head_dim : 2 * head_dim, where] = turned.astype(jnp.bfloat16)
            values = gv_ref[tile].T * proj_scale
            grad_ref[0, 2 * head_dim :, where] = values.astype(jnp.bfloat16)
            return carry

        lax.fori_loop(0, tiles, keys, 0)


def attention(group, queries, keys, values, grads, cosine, sine, width):
    first, count = group
    _, seq_len, head_dim = queries.shape
    block = min(BLOCK, seq_len)
    tile_len = min(TILE, block)
    tiles = seq_len // tile_len
    of_head = pl.BlockSpec((1, seq_len, head_dim), lambda h, i: (first + h, 0, 0))
    table = pl.BlockSpec((seq_len, head_dim), lambda h, i: (0, 0))
    return pl.pallas_call(
        partial(attention_kernel, 1.0 / math.sqrt(head_dim), 1.0 / math.sqrt(width)),
        grid=(count, seq_len // block),
        in_specs=[of_head] * 4 + [table] * 2,
        out_specs=[
            pl.BlockSpec((1, 3 * head_dim, seq_len), lambda h, i: (h, 0, 0)),
            pl.BlockSpec((1, head_dim, seq_len), lambda h, i: (h, 0, 0)),
        ],
        out_shape=[
            jax.ShapeDtypeStruct((count, 3 * head_dim, seq_len), jnp.bfloat16),
            jax.ShapeDtypeStruct((count, head_dim, seq_len), jnp.bfloat16),
        ],
        scratch_shapes=[pltpu.VMEM((tiles, tile_len, block), jnp.float32)] * 3
        + [pltpu.VMEM((tiles, head_dim, tile_len), jnp.bfloat16)] * 2
        + [pltpu.VMEM((tiles, tile_len, head_dim), jnp.float32)] * 2,
        compiler_params=params(),
        cost_estimate=SHORT,
        name="attention",
    )(queries, keys, values, grads, cosine, sine)


def momenta_kernel(
    scale, grad_ref, att_ref, normed_ref, rows_ref, mqkv_ref, mout_ref, moved_ref
):
    count, three, _ = grad_ref.shape

    def of_head(head, carry):
        def chunk(here):
            grad = product(grad_ref[head], normed_ref[:, here]).T.astype(jnp.bfloat16)
            moved = BETA * mqkv_ref[head, here, :].astype(jnp.float32) + grad.astype(jnp.float32)
            moved_ref[head, here, :three] = moved.astype(jnp.bfloat16)
            grad = (product(att_ref[head], rows_ref[:, here]) * scale).astype(jnp.bfloat16)
            moved = BETA * mout_ref[head, :, here].astype(jnp.float32) + grad.astype(jnp.float32)
            moved_ref[head, here, three:] = moved.T.astype(jnp.bfloat16)

        in_chunks(moved_ref.shape[1], CHUNK, chunk)
        return carry

    lax.fori_loop(0, count, of_head, 0)


def momenta(group, piece, grad_proj, attended, normed, rows, mom_qkv, mom_out, scale):
    first, count, block = piece
    start, heads = group
    seq_len = normed.shape[0]
    three, head_dim = grad_proj.shape[1], attended.shape[1]
    group_index = start // heads
    return pl.pallas_call(
        partial(momenta_kernel, scale),
        grid=(count,),
        in_specs=[
            pl.BlockSpec((heads, three, seq_len), lambda i: (0, 0, 0)),
            pl.BlockSpec((heads, head_dim, seq_len), lambda i: (0, 0, 0)),
            pl.BlockSpec((seq_len, block), lambda i: (0, first + i)),
            pl.BlockSpec((seq_len, block), lambda i: (0, first + i)),
            pl.BlockSpec((heads, block, three), lambda i: (group_index, first + i, 0)),
            pl.BlockSpec((heads, head_dim, block), lambda i: (group_index, 0, first + i)),
        ],
        out_specs=pl.BlockSpec((heads, block, three + head_dim), lambda i: (0, i, 0)),
        out_shape=jax.ShapeDtypeStruct((heads, count * block, three + head_dim), jnp.bfloat16),
        compiler_params=params(),
        cost_estimate=SHORT,
        name="momenta",
    )(grad_proj, attended, normed, rows, mom_qkv, mom_out)


def average_kernel(rate_ref, qkv, other_qkv, out, other_out, moment, other_moment, *refs):
    rate = rate_ref[0, 0]
    new_qkv, new_out, new_mom_qkv, new_mom_out = refs[-4:]
    three = qkv.shape[-1]

    def halfway(own, other):
        return ((own.astype(jnp.float32) + other.astype(jnp.float32)) * 0.5).astype(jnp.bfloat16)

    def moved(weight, moment):
        new = weight.astype(jnp.float32) - rate * moment.astype(jnp.float32)
        return new.astype(jnp.bfloat16)

    def chunk(here):
        own, other = moment[0, here, :three], other_moment[0, here, :three]
        new = halfway(moved(qkv[0, 0, here, :], own), moved(other_qkv[0, 0, here, :], other))
        new_qkv[0, 0, here, :] = new
        new_mom_qkv[0, 0, here, :] = halfway(own, other)
        own = moment[0, here, three:].astype(jnp.float32).T
        other = other_moment[0, here, three:].astype(jnp.float32).T
        new = halfway(moved(out[0, 0, :, here], own), moved(other_out[0, 0, :, here], other))
        new_out[0, 0, :, here] = new
        new_mom_out[0, 0, :, here] = halfway(own, other)

    in_chunks(moment.shape[1], 128, chunk)


def average(group, piece, rate, own, other, moment, other_moment, previous):
    first, count, block = piece
    start, heads = group
    (qkv, out), (other_qkv, other_out) = own, other
    three, head_dim = qkv.shape[-1], out.shape[2]
    high = pl.BlockSpec((1, 1, block, three), lambda h, i: (0, start + h, first + i, 0))
    wide = pl.BlockSpec((1, 1, head_dim, block), lambda h, i: (0, start + h, 0, first + i))
    packed = pl.BlockSpec((1, block, three + head_dim), lambda h, i: (h, i, 0))
    in_specs = [pl.BlockSpec(memory_space=pltpu.SMEM), high, high, wide, wide, packed, packed]
    args = [rate, qkv, other_qkv, out, other_out, moment, other_moment]
    aliases = {}
    if previous is not None:
        aliases = {len(args) + i: i for i in range(4)}
        args += list(previous)
        in_specs += [pl.BlockSpec(memory_space=pl.ANY)] * 4
    return pl.pallas_call(
        average_kernel,
        grid=(heads, count),
        in_specs=in_specs,
        out_specs=[high, wide] * 2,
        out_shape=[jax.ShapeDtypeStruct(w.shape, jnp.bfloat16) for w in own] * 2,
        input_output_aliases=aliases,
        compiler_params=params(),
        cost_estimate=SHORT,
        name="average",
    )(*args)


def pieces_of(last, width):
    if not last or width % BLOCK or width < 2 * BLOCK:
        block = min(BLOCK, width)
        return [(0, width // block, block)]
    return [(0, width // BLOCK - 1, BLOCK), (width // BLOCK - 1, 1, BLOCK)]


def update(by, inputs, out_grad, norm_gain, w_qkv, w_out, mom_qkv, mom_out, rate):
    own = (w_qkv, w_out)
    other_qkv = shifted(w_qkv, by)

    devices = lax.axis_size("fsdp")
    blocks = exchanged([normalised(inputs, norm_gain, part) for part in range(PARTS)], 0)
    row_blocks = exchanged([out_grad], 0)
    stage = 1
    while len(blocks) < devices * PARTS:
        blocks = exchanged(blocks, stage)
        stage += 1
    normed = assembled(blocks)
    other_out = shifted(w_out, by)
    w_qkv, w_out = w_qkv[0], w_out[0]

    seq_len, width = normed.shape
    heads, head_dim, _ = w_out.shape
    out_scale = 1.0 / math.sqrt(HEADS * head_dim)
    tables = rotary_tables(seq_len, head_dim)
    parts = project(normed, w_qkv, *tables)
    row_blocks[-1], parts = lax.optimization_barrier((row_blocks[-1], parts))
    stage = 1
    while len(row_blocks) < devices:
        row_blocks = exchanged(row_blocks, stage)
        stage += 1
    rows = assembled(row_blocks)
    grads = cotangent(rows, w_out, out_scale)

    made = []
    some = max(heads // 2, 1)
    for start in range(0, heads, some):
        group = (start, some)
        grad_proj, attended = attention(group, *parts, grads, *tables, width)
        if start == 0:
            grad_proj, other_qkv = lax.optimization_barrier((grad_proj, other_qkv))
        if start + some == heads:
            grad_proj, other_out = lax.optimization_barrier((grad_proj, other_out))
        for piece in pieces_of(start + some == heads, width):
            moment = momenta(
                group, piece, grad_proj, attended, normed, rows, mom_qkv, mom_out, out_scale
            )
            grads, normed, moment = lax.optimization_barrier((grads, normed, moment))
            made.append((group, piece, moment, shifted(moment, by)))
    results, other = None, (other_qkv, other_out)
    for group, piece, moment, other_moment in made:
        results = average(group, piece, rate, own, other, moment, other_moment, results)
    return tuple(results)


def per_device(inputs, out_grad, norm_gain, w_qkv, w_out, mom_qkv, mom_out, step_index):
    rate = RATE * (step_index[0].astype(jnp.float32) + 1.0) / (4.0 * LEVELS)
    exponent = jnp.remainder(step_index[0], LEVELS)
    return lax.switch(
        exponent,
        [partial(update, 1 << level) for level in range(LEVELS)],
        inputs[0],
        out_grad[0],
        norm_gain,
        w_qkv,
        w_out,
        mom_qkv[0],
        mom_out[0],
        rate.reshape(1, 1),
    )


def solution(mesh):
    return jax.shard_map(
        per_device,
        mesh=mesh,
        in_specs=(
            P("gossip", "fsdp", None),
            P("gossip", "fsdp", None),
            P("gossip", None),
            P("gossip", "fsdp", None, None),
            P("gossip", "fsdp", None, None),
            P("gossip", "fsdp", None, None),
            P("gossip", "fsdp", None, None),
            P(),
        ),
        out_specs=(
            P("gossip", "fsdp", None, None),
            P("gossip", "fsdp", None, None),
            P("gossip", "fsdp", None, None),
            P("gossip", "fsdp", None, None),
        ),
        check_vma=False,
    )
```

```python
from functools import partial
import math

import jax
import jax.numpy as jnp
from jax import lax
from jax.experimental import pallas as pl
from jax.experimental.pallas import tpu as pltpu
from jax.sharding import PartitionSpec as P

HEADS = 16
LEVELS = 3

BETA = 0.9
RATE = 0.1
EPSILON = 1e-05

VMEM_LIMIT = 65280 * 1024
BLOCK = 512
CHUNK = 256
TILE = 512
PARTS = 2

SHORT = pl.CostEstimate(flops=1, bytes_accessed=1, transcendentals=0)


def product(left, right, left_dim=1, right_dim=0):
    return lax.dot_general(
        left, right, (((left_dim,), (right_dim,)), ((), ())), preferred_element_type=jnp.float32
    )


def in_chunks(size, chunk, body):
    chunk = min(chunk, size)

    def step(index, carry):
        body(pl.ds(pl.multiple_of(index * chunk, chunk), chunk))
        return carry

    lax.fori_loop(0, size // chunk, step, 0)


def params():
    return pltpu.CompilerParams(vmem_limit_bytes=VMEM_LIMIT)


def shifted(value, by):
    size = lax.axis_size("gossip")
    return lax.ppermute(value, "gossip", [(i, (i + by) % size) for i in range(size)])


def exchanged(blocks, stage):
    size = lax.axis_size("fsdp")
    bit = size >> (stage + 1)
    pairs = [(i, i ^ bit) for i in range(size)]
    return blocks + [lax.ppermute(block, "fsdp", pairs) for block in blocks]


def places_of(size, parts):
    places, bit = [(0, part) for part in range(parts)], size // 2
    while bit:
        places += [(offset ^ bit, part) for offset, part in places]
        bit //= 2
    return places


def assemble_kernel(places, *refs):
    blocks, (out_ref, held, came, left) = refs[:-4], refs[-4:]
    me = lax.axis_index("fsdp")
    high = blocks[0].shape[0]
    inward, outward = [], []
    parts = 1 + max(part for _, part in places)
    for number, ((offset, part), block) in enumerate(zip(places, blocks)):
        place = pl.ds(pl.multiple_of(((me ^ offset) * parts + part) * high, high), high)
        inward.append(pltpu.make_async_copy(block, held.at[number], came.at[number]))
        outward.append(
            pltpu.make_async_copy(held.at[number], out_ref.at[place, :], left.at[number])
        )
        inward[-1].start()
    for first, second in zip(inward, outward):
        first.wait()
        second.start()
    for copy in outward:
        copy.wait()


def assembled(blocks):
    size, devices = len(blocks), lax.axis_size("fsdp")
    high, wide = blocks[0].shape
    return pl.pallas_call(
        partial(assemble_kernel, places_of(devices, size // devices)),
        in_specs=[pl.BlockSpec(memory_space=pl.ANY)] * size,
        out_specs=pl.BlockSpec(memory_space=pl.ANY),
        out_shape=jax.ShapeDtypeStruct((size * high, wide), blocks[0].dtype),
        scratch_shapes=[
            pltpu.VMEM((size, high, wide), blocks[0].dtype),
            pltpu.SemaphoreType.DMA((size,)),
            pltpu.SemaphoreType.DMA((size,)),
        ],
        compiler_params=params(),
        cost_estimate=SHORT,
        name="assemble",
    )(*blocks)


def rotary_tables(seq_len, head_dim):
    half = head_dim // 2
    column = jnp.arange(head_dim)
    frequency = jnp.exp(
        -math.log(10000.0) * 2.0 * (column % half).astype(jnp.float32) / head_dim
    )
    angles = jnp.arange(seq_len).astype(jnp.float32)[:, None] * frequency[None, :]
    sign = jnp.where(column < half, -1.0, 1.0)
    return jnp.cos(angles), jnp.sin(angles) * sign[None, :]


def norm_kernel(rows_ref, gain_ref, out_ref):
    def chunk(here):
        rows = rows_ref[here, :].astype(jnp.float32)
        stats = lax.rsqrt(jnp.mean(rows * rows, -1, keepdims=True) + EPSILON)
        out_ref[here, :] = (rows * stats * gain_ref[...]).astype(jnp.bfloat16)

    in_chunks(rows_ref.shape[0], 64, chunk)


def normalised(rows, gain, part):
    high, wide = rows.shape
    block = high // PARTS
    return pl.pallas_call(
        norm_kernel,
        grid=(1,),
        in_specs=[
            pl.BlockSpec((block, wide), lambda i: (part, 0)),
            pl.BlockSpec((1, wide), lambda i: (0, 0)),
        ],
        out_specs=pl.BlockSpec((block, wide), lambda i: (0, 0)),
        out_shape=jax.ShapeDtypeStruct((block, wide), jnp.bfloat16),
        compiler_params=params(),
        cost_estimate=SHORT,
        name="normalised",
    )(rows, gain)


def project_kernel(scale, rows_ref, weight_ref, cos_ref, sin_ref, q_ref, k_ref, v_ref):
    width = cos_ref.shape[-1]

    def of_head(head, carry):
        def chunk(here):
            cosine, sine = cos_ref[here, :], sin_ref[here, :]
            projected = product(rows_ref[here, :], weight_ref[head]) * scale
            for which, out_ref in enumerate((q_ref, k_ref)):
                part = projected[:, which * width : (which + 1) * width]
                turned = part * cosine + pltpu.roll(part, width // 2, 1) * sine
                out_ref[head, here, :] = turned.astype(jnp.bfloat16)
            v_ref[head, here, :] = projected[:, 2 * width :].astype(jnp.bfloat16)

        in_chunks(rows_ref.shape[0], CHUNK, chunk)
        return carry

    lax.fori_loop(0, weight_ref.shape[0], of_head, 0)


def project(rows, weights, cosine, sine):
    seq_len, width = rows.shape
    heads, _, three = weights.shape
    head_dim = three // 3
    block = min(BLOCK, seq_len)
    table = pl.BlockSpec((block, head_dim), lambda i: (i, 0))
    return pl.pallas_call(
        partial(project_kernel, 1.0 / math.sqrt(width)),
        grid=(seq_len // block,),
        in_specs=[
            pl.BlockSpec((block, width), lambda i: (i, 0)),
            pl.BlockSpec((heads, width, three), lambda i: (0, 0, 0)),
            table,
            table,
        ],
        out_specs=[pl.BlockSpec((heads, block, head_dim), lambda i: (0, i, 0))] * 3,
        out_shape=[jax.ShapeDtypeStruct((heads, seq_len, head_dim), jnp.bfloat16)] * 3,
        compiler_params=params(),
        cost_estimate=SHORT,
        name="project",
    )(rows, weights, cosine, sine)


def cotangent_kernel(scale, rows_ref, weight_ref, out_ref):
    heads, head_dim, width = weight_ref.shape
    some = math.gcd(heads, 2)

    def of_heads(index, carry):
        first = index * some
        weights = weight_ref[pl.ds(first, some)].reshape(some * head_dim, width)
        grads = (product(rows_ref[...], weights, 1, 1) * scale).astype(jnp.bfloat16)
        for number in range(some):
            out_ref[first + number] = grads[:, number * head_dim : (number + 1) * head_dim]
        return carry

    lax.fori_loop(0, heads // some, of_heads, 0)


def cotangent(rows, weights, scale):
    seq_len, width = rows.shape
    heads, head_dim, _ = weights.shape
    block = min(BLOCK, seq_len)
    return pl.pallas_call(
        partial(cotangent_kernel, scale),
        grid=(seq_len // block,),
        in_specs=[
            pl.BlockSpec((block, width), lambda i: (i, 0)),
            pl.BlockSpec((heads, head_dim, width), lambda i: (0, 0, 0)),
        ],
        out_specs=pl.BlockSpec((heads, block, head_dim), lambda i: (0, i, 0)),
        out_shape=jax.ShapeDtypeStruct((heads, seq_len, head_dim), jnp.bfloat16),
        compiler_params=params(),
        cost_estimate=SHORT,
        name="cotangent",
    )(rows, weights)


def folded(values, combine):
    rows, columns = values.shape
    return combine(values.reshape(rows // 8, 8, columns), 0)


def attention_kernel(
    scale,
    proj_scale,
    q_ref,
    k_ref,
    v_ref,
    g_ref,
    cos_ref,
    sin_ref,
    grad_ref,
    att_ref,
    s_ref,
    p_ref,
    d_ref,
    kt_ref,
    vt_ref,
    gk_ref,
    gv_ref,
):
    step = pl.program_id(1)
    _, tile_len, block = s_ref.shape
    head_dim = q_ref.shape[-1]
    half = head_dim // 2
    in_block = block // tile_len

    def rows(tile):
        return pl.ds(pl.multiple_of(tile * tile_len, tile_len), tile_len)

    here = pl.ds(pl.multiple_of(step * block, block), block)
    queries = q_ref[0, here, :]
    grads = g_ref[0, here, :]
    first_tile, tiles = step * in_block, (step + 1) * in_block

    def enter(tile, carry):
        kt_ref[tile] = k_ref[0, rows(tile), :].T
        vt_ref[tile] = v_ref[0, rows(tile), :].T
        gk_ref[tile] = jnp.zeros(gk_ref.shape[1:], jnp.float32)
        gv_ref[tile] = jnp.zeros(gv_ref.shape[1:], jnp.float32)
        return carry

    lax.fori_loop(first_tile, tiles, enter, 0)

    behind = lax.broadcasted_iota(jnp.int32, (tile_len, block), 0) - lax.broadcasted_iota(
        jnp.int32, (tile_len, block), 1
    )

    def score(tile, top):
        scores = product(k_ref[0, rows(tile), :], queries, 1, 1)
        scores = jnp.where(behind <= step * block - tile * tile_len, scores, -jnp.inf)
        s_ref[tile] = scores
        return jnp.maximum(top, folded(scores, jnp.max))

    top = lax.fori_loop(0, tiles, score, jnp.full((8, block), -jnp.inf, jnp.float32))
    factor = scale * math.log2(math.e)
    top = jnp.max(top, 0, keepdims=True) * factor

    def weigh(tile, sums):
        total, inner = sums
        weights = jnp.exp2(s_ref[tile] * factor - top)
        grad_probs = product(v_ref[0, rows(tile), :], grads, 1, 1)
        p_ref[tile] = weights
        d_ref[tile] = grad_probs
        return total + folded(weights, jnp.sum), inner + folded(weights * grad_probs, jnp.sum)

    zeros = jnp.zeros((8, block), jnp.float32)
    total, inner = lax.fori_loop(0, tiles, weigh, (zeros, zeros))
    inverse = 1.0 / jnp.sum(total, 0, keepdims=True)
    inner = jnp.sum(inner, 0, keepdims=True) * inverse

    def back(tile, sums):
        att, grad_q = sums
        probs = p_ref[tile] * inverse
        probs_b = probs.astype(jnp.bfloat16)
        grad_scores = (probs * (d_ref[tile] - inner)).astype(jnp.bfloat16)
        gv_ref[tile] += product(probs_b, grads)
        gk_ref[tile] += product(grad_scores, queries)
        return att + product(vt_ref[tile], probs_b), grad_q + product(kt_ref[tile], grad_scores)

    zeros = jnp.zeros((head_dim, block), jnp.float32)
    att, grad_q = lax.fori_loop(0, tiles, back, (zeros, zeros))

    att_ref[0, :, here] = att.astype(jnp.bfloat16)
    cosine, sine = cos_ref[here, :].T, sin_ref[here, :].T
    turned = grad_q * cosine - pltpu.roll(grad_q, half, 0) * sine
    grad_ref[0, :head_dim, here] = (turned * (scale * proj_scale)).astype(jnp.bfloat16)

    @pl.when(step == pl.num_programs(1) - 1)
    def finish():
        def keys(tile, carry):
            where = rows(tile)
            grad_k = gk_ref[tile]
            turned = grad_k * cos_ref[where, :] - pltpu.roll(grad_k, half, 1) * sin_ref[where, :]
            turned = (turned * (scale * proj_scale)).T
            grad_ref[0, head_dim : 2 * head_dim, where] = turned.astype(jnp.bfloat16)
            values = gv_ref[tile].T * proj_scale
            grad_ref[0, 2 * head_dim :, where] = values.astype(jnp.bfloat16)
            return carry

        lax.fori_loop(0, tiles, keys, 0)


def attention(group, queries, keys, values, grads, cosine, sine, width):
    first, count = group
    _, seq_len, head_dim = queries.shape
    block = min(BLOCK, seq_len)
    tile_len = min(TILE, block)
    tiles = seq_len // tile_len
    of_head = pl.BlockSpec((1, seq_len, head_dim), lambda h, i: (first + h, 0, 0))
    table = pl.BlockSpec((seq_len, head_dim), lambda h, i: (0, 0))
    return pl.pallas_call(
        partial(attention_kernel, 1.0 / math.sqrt(head_dim), 1.0 / math.sqrt(width)),
        grid=(count, seq_len // block),
        in_specs=[of_head] * 4 + [table] * 2,
        out_specs=[
            pl.BlockSpec((1, 3 * head_dim, seq_len), lambda h, i: (h, 0, 0)),
            pl.BlockSpec((1, head_dim, seq_len), lambda h, i: (h, 0, 0)),
        ],
        out_shape=[
            jax.ShapeDtypeStruct((count, 3 * head_dim, seq_len), jnp.bfloat16),
            jax.ShapeDtypeStruct((count, head_dim, seq_len), jnp.bfloat16),
        ],
        scratch_shapes=[pltpu.VMEM((tiles, tile_len, block), jnp.float32)] * 3
        + [pltpu.VMEM((tiles, head_dim, tile_len), jnp.bfloat16)] * 2
        + [pltpu.VMEM((tiles, tile_len, head_dim), jnp.float32)] * 2,
        compiler_params=params(),
        cost_estimate=SHORT,
        name="attention",
    )(queries, keys, values, grads, cosine, sine)


def momenta_kernel(
    scale, grad_ref, att_ref, normed_ref, rows_ref, mqkv_ref, mout_ref, *refs
):
    outs, moved_ref = refs[:-1], refs[-1]
    count, three, _ = grad_ref.shape

    def of_head(head, carry):
        def chunk(here):
            grad = product(grad_ref[head], normed_ref[:, here]).T.astype(jnp.bfloat16)
            moved = BETA * mqkv_ref[head, here, :].astype(jnp.float32) + grad.astype(jnp.float32)
            moved_ref[head, here, :three] = moved.astype(jnp.bfloat16)
            grad = (product(att_ref[head], rows_ref[:, here]) * scale).astype(jnp.bfloat16)
            moved = BETA * mout_ref[head, :, here].astype(jnp.float32) + grad.astype(jnp.float32)
            moved_ref[head, here, three:] = moved.T.astype(jnp.bfloat16)

        in_chunks(moved_ref.shape[1], CHUNK, chunk)
        return carry

    lax.fori_loop(0, count, of_head, 0)
    for number, out_ref in enumerate(outs if len(refs) > 1 else ()):

        @pl.when(pl.program_id(0) == number)
        def hand_out(out_ref=out_ref):
            def copy(here):
                out_ref[:, here, :] = moved_ref[:, here, :]

            in_chunks(out_ref.shape[1], 32, copy)


def momenta(group, piece, apart, grad_proj, attended, normed, rows, mom_qkv, mom_out, scale):
    first, count, block = piece
    start, heads = group
    seq_len = normed.shape[0]
    three, head_dim = grad_proj.shape[1], attended.shape[1]
    group_index = start // heads
    packed = (heads, block, three + head_dim)
    if apart:
        out_specs = [pl.BlockSpec(packed, lambda i: (0, 0, 0))] * count
        out_shape = [jax.ShapeDtypeStruct(packed, jnp.bfloat16)] * count
    else:
        out_specs = pl.BlockSpec(packed, lambda i: (0, i, 0))
        out_shape = jax.ShapeDtypeStruct((heads, count * block, packed[-1]), jnp.bfloat16)
    return pl.pallas_call(
        partial(momenta_kernel, scale),
        grid=(count,),
        in_specs=[
            pl.BlockSpec((heads, three, seq_len), lambda i: (0, 0, 0)),
            pl.BlockSpec((heads, head_dim, seq_len), lambda i: (0, 0, 0)),
            pl.BlockSpec((seq_len, block), lambda i: (0, first + i)),
            pl.BlockSpec((seq_len, block), lambda i: (0, first + i)),
            pl.BlockSpec((heads, block, three), lambda i: (group_index, first + i, 0)),
            pl.BlockSpec((heads, head_dim, block), lambda i: (group_index, 0, first + i)),
        ],
        out_specs=out_specs,
        out_shape=out_shape,
        scratch_shapes=[pltpu.VMEM(packed, jnp.bfloat16)] if apart else [],
        compiler_params=params(),
        cost_estimate=SHORT,
        name="momenta",
    )(grad_proj, attended, normed, rows, mom_qkv, mom_out)


def average_kernel(rate_ref, qkv, other_qkv, out, other_out, moment, other_moment, *refs):
    rate = rate_ref[0, 0]
    new_qkv, new_out, new_mom_qkv, new_mom_out = refs[-4:]
    three = qkv.shape[-1]

    def halfway(own, other):
        return ((own.astype(jnp.float32) + other.astype(jnp.float32)) * 0.5).astype(jnp.bfloat16)

    def moved(weight, moment):
        new = weight.astype(jnp.float32) - rate * moment.astype(jnp.float32)
        return new.astype(jnp.bfloat16)

    def chunk(here):
        own, other = moment[0, here, :three], other_moment[0, here, :three]
        new = halfway(moved(qkv[0, 0, here, :], own), moved(other_qkv[0, 0, here, :], other))
        new_qkv[0, 0, here, :] = new
        new_mom_qkv[0, 0, here, :] = halfway(own, other)
        own = moment[0, here, three:].T
        other = other_moment[0, here, three:].T
        new = halfway(moved(out[0, 0, :, here], own), moved(other_out[0, 0, :, here], other))
        new_out[0, 0, :, here] = new
        new_mom_out[0, 0, :, here] = halfway(own, other)

    in_chunks(moment.shape[1], 128, chunk)


def average(group, piece, rate, own, other, moment, other_moment, previous):
    first, count, block = piece
    start, heads = group
    (qkv, out), (other_qkv, other_out) = own, other
    three, head_dim = qkv.shape[-1], out.shape[2]
    high = pl.BlockSpec((1, 1, block, three), lambda h, i: (0, start + h, first + i, 0))
    wide = pl.BlockSpec((1, 1, head_dim, block), lambda h, i: (0, start + h, 0, first + i))
    packed = pl.BlockSpec((1, block, three + head_dim), lambda h, i: (h, i, 0))
    in_specs = [pl.BlockSpec(memory_space=pltpu.SMEM), high, high, wide, wide, packed, packed]
    args = [rate, qkv, other_qkv, out, other_out, moment, other_moment]
    aliases = {}
    if previous is not None:
        aliases = {len(args) + i: i for i in range(4)}
        args += list(previous)
        in_specs += [pl.BlockSpec(memory_space=pl.ANY)] * 4
    return pl.pallas_call(
        average_kernel,
        grid=(heads, count),
        in_specs=in_specs,
        out_specs=[high, wide] * 2,
        out_shape=[jax.ShapeDtypeStruct(w.shape, jnp.bfloat16) for w in own] * 2,
        input_output_aliases=aliases,
        compiler_params=params(),
        cost_estimate=SHORT,
        name="average",
    )(*args)


def pieces_of(last, width):
    if not last or width % BLOCK or width < 2 * BLOCK:
        block = min(BLOCK, width)
        return [(0, width // block, block, False)]
    chunks = width // CHUNK
    return [(0, width // BLOCK - 1, BLOCK, False), (chunks - 2, 2, CHUNK, True)]


def update(by, inputs, out_grad, norm_gain, w_qkv, w_out, mom_qkv, mom_out, rate):
    own = (w_qkv, w_out)
    other_qkv = shifted(w_qkv, by)

    devices = lax.axis_size("fsdp")
    blocks = exchanged([normalised(inputs, norm_gain, part) for part in range(PARTS)], 0)
    row_blocks = exchanged([out_grad], 0)
    stage = 1
    while len(blocks) < devices * PARTS:
        blocks = exchanged(blocks, stage)
        stage += 1
    normed = assembled(blocks)
    other_out = shifted(w_out, by)
    w_qkv, w_out = w_qkv[0], w_out[0]

    seq_len, width = normed.shape
    heads, head_dim, _ = w_out.shape
    out_scale = 1.0 / math.sqrt(HEADS * head_dim)
    tables = rotary_tables(seq_len, head_dim)
    parts = project(normed, w_qkv, *tables)
    row_blocks[-1], parts = lax.optimization_barrier((row_blocks[-1], parts))
    stage = 1
    while len(row_blocks) < devices:
        row_blocks = exchanged(row_blocks, stage)
        stage += 1
    rows = assembled(row_blocks)
    grads = cotangent(rows, w_out, out_scale)

    made = []
    some = max(heads // 2, 1)
    for start in range(0, heads, some):
        group = (start, some)
        grad_proj, attended = attention(group, *parts, grads, *tables, width)
        if start == 0:
            grad_proj, other_qkv = lax.optimization_barrier((grad_proj, other_qkv))
        if start + some == heads:
            grad_proj, other_out = lax.optimization_barrier((grad_proj, other_out))
        for first, count, block, apart in pieces_of(start + some == heads, width):
            piece = (first, count, block)
            moment = momenta(
                group, piece, apart, grad_proj, attended, normed, rows, mom_qkv, mom_out, out_scale
            )
            grads, normed, moment = lax.optimization_barrier((grads, normed, moment))
            if apart:
                for number, part in enumerate(moment):
                    made.append((group, (first + number, 1, block), part, shifted(part, by)))
            else:
                made.append((group, piece, moment, shifted(moment, by)))
    results, other = None, (other_qkv, other_out)
    for group, piece, moment, other_moment in made:
        results = average(group, piece, rate, own, other, moment, other_moment, results)
    return tuple(results)


def per_device(inputs, out_grad, norm_gain, w_qkv, w_out, mom_qkv, mom_out, step_index):
    rate = RATE * (step_index[0].astype(jnp.float32) + 1.0) / (4.0 * LEVELS)
    exponent = jnp.remainder(step_index[0], LEVELS)
    return lax.switch(
        exponent,
        [partial(update, 1 << level) for level in range(LEVELS)],
        inputs[0],
        out_grad[0],
        norm_gain,
        w_qkv,
        w_out,
        mom_qkv[0],
        mom_out[0],
        rate.reshape(1, 1),
    )


def solution(mesh):
    return jax.shard_map(
        per_device,
        mesh=mesh,
        in_specs=(
            P("gossip", "fsdp", None),
            P("gossip", "fsdp", None),
            P("gossip", None),
            P("gossip", "fsdp", None, None),
            P("gossip", "fsdp", None, None),
            P("gossip", "fsdp", None, None),
            P("gossip", "fsdp", None, None),
            P(),
        ),
        out_specs=(
            P("gossip", "fsdp", None, None),
            P("gossip", "fsdp", None, None),
            P("gossip", "fsdp", None, None),
            P("gossip", "fsdp", None, None),
        ),
        check_vma=False,
    )
```

```python
from functools import partial
import math

import jax
import jax.numpy as jnp
from jax import lax
from jax.experimental import pallas as pl
from jax.experimental.pallas import tpu as pltpu
from jax.sharding import PartitionSpec as P

HEADS = 16
LEVELS = 3

BETA = 0.9
RATE = 0.1
EPSILON = 1e-05

VMEM_LIMIT = 65408 * 1024
BLOCK = 512
CHUNK = 256
TILE = 512
PARTS = 2

SHORT = pl.CostEstimate(flops=1, bytes_accessed=1, transcendentals=0)


def product(left, right, left_dim=1, right_dim=0):
    return lax.dot_general(
        left, right, (((left_dim,), (right_dim,)), ((), ())), preferred_element_type=jnp.float32
    )


def in_chunks(size, chunk, body):
    chunk = min(chunk, size)

    def step(index, carry):
        body(pl.ds(pl.multiple_of(index * chunk, chunk), chunk))
        return carry

    lax.fori_loop(0, size // chunk, step, 0)


def params():
    return pltpu.CompilerParams(vmem_limit_bytes=VMEM_LIMIT)


def shifted(value, by):
    size = lax.axis_size("gossip")
    return lax.ppermute(value, "gossip", [(i, (i + by) % size) for i in range(size)])


def exchanged(blocks, stage):
    size = lax.axis_size("fsdp")
    bit = size >> (stage + 1)
    pairs = [(i, i ^ bit) for i in range(size)]
    return blocks + [lax.ppermute(block, "fsdp", pairs) for block in blocks]


def places_of(size, parts):
    places, bit = [(0, part) for part in range(parts)], size // 2
    while bit:
        places += [(offset ^ bit, part) for offset, part in places]
        bit //= 2
    return places


def assemble_kernel(places, *refs):
    blocks, (out_ref, held, came, left) = refs[:-4], refs[-4:]
    me = lax.axis_index("fsdp")
    high = blocks[0].shape[0]
    inward, outward = [], []
    parts = 1 + max(part for _, part in places)
    for number, ((offset, part), block) in enumerate(zip(places, blocks)):
        place = pl.ds(pl.multiple_of(((me ^ offset) * parts + part) * high, high), high)
        inward.append(pltpu.make_async_copy(block, held.at[number], came.at[number]))
        outward.append(
            pltpu.make_async_copy(held.at[number], out_ref.at[place, :], left.at[number])
        )
        inward[-1].start()
    for first, second in zip(inward, outward):
        first.wait()
        second.start()
    for copy in outward:
        copy.wait()


def assembled(blocks):
    size, devices = len(blocks), lax.axis_size("fsdp")
    high, wide = blocks[0].shape
    return pl.pallas_call(
        partial(assemble_kernel, places_of(devices, size // devices)),
        in_specs=[pl.BlockSpec(memory_space=pl.ANY)] * size,
        out_specs=pl.BlockSpec(memory_space=pl.ANY),
        out_shape=jax.ShapeDtypeStruct((size * high, wide), blocks[0].dtype),
        scratch_shapes=[
            pltpu.VMEM((size, high, wide), blocks[0].dtype),
            pltpu.SemaphoreType.DMA((size,)),
            pltpu.SemaphoreType.DMA((size,)),
        ],
        compiler_params=params(),
        cost_estimate=SHORT,
        name="assemble",
    )(*blocks)


def rotary_tables(seq_len, head_dim):
    half = head_dim // 2
    column = jnp.arange(head_dim)
    frequency = jnp.exp(
        -math.log(10000.0) * 2.0 * (column % half).astype(jnp.float32) / head_dim
    )
    angles = jnp.arange(seq_len).astype(jnp.float32)[:, None] * frequency[None, :]
    sign = jnp.where(column < half, -1.0, 1.0)
    return jnp.cos(angles), jnp.sin(angles) * sign[None, :]


def norm_kernel(rows_ref, gain_ref, out_ref):
    def chunk(here):
        rows = rows_ref[here, :].astype(jnp.float32)
        stats = lax.rsqrt(jnp.mean(rows * rows, -1, keepdims=True) + EPSILON)
        out_ref[here, :] = (rows * stats * gain_ref[...]).astype(jnp.bfloat16)

    in_chunks(rows_ref.shape[0], 64, chunk)


def normalised(rows, gain, part):
    high, wide = rows.shape
    block = high // PARTS
    return pl.pallas_call(
        norm_kernel,
        grid=(1,),
        in_specs=[
            pl.BlockSpec((block, wide), lambda i: (part, 0)),
            pl.BlockSpec((1, wide), lambda i: (0, 0)),
        ],
        out_specs=pl.BlockSpec((block, wide), lambda i: (0, 0)),
        out_shape=jax.ShapeDtypeStruct((block, wide), jnp.bfloat16),
        compiler_params=params(),
        cost_estimate=SHORT,
        name="normalised",
    )(rows, gain)


def project_kernel(scale, rows_ref, weight_ref, cos_ref, sin_ref, q_ref, k_ref, v_ref):
    width = cos_ref.shape[-1]

    def of_head(head, carry):
        def chunk(here):
            cosine, sine = cos_ref[here, :], sin_ref[here, :]
            projected = product(rows_ref[here, :], weight_ref[head]) * scale
            for which, out_ref in enumerate((q_ref, k_ref)):
                part = projected[:, which * width : (which + 1) * width]
                turned = part * cosine + pltpu.roll(part, width // 2, 1) * sine
                out_ref[head, here, :] = turned.astype(jnp.bfloat16)
            v_ref[head, here, :] = projected[:, 2 * width :].astype(jnp.bfloat16)

        in_chunks(rows_ref.shape[0], CHUNK, chunk)
        return carry

    lax.fori_loop(0, weight_ref.shape[0], of_head, 0)


def project(rows, weights, cosine, sine):
    seq_len, width = rows.shape
    heads, _, three = weights.shape
    head_dim = three // 3
    block = min(BLOCK, seq_len)
    table = pl.BlockSpec((block, head_dim), lambda i: (i, 0))
    return pl.pallas_call(
        partial(project_kernel, 1.0 / math.sqrt(width)),
        grid=(seq_len // block,),
        in_specs=[
            pl.BlockSpec((block, width), lambda i: (i, 0)),
            pl.BlockSpec((heads, width, three), lambda i: (0, 0, 0)),
            table,
            table,
        ],
        out_specs=[pl.BlockSpec((heads, block, head_dim), lambda i: (0, i, 0))] * 3,
        out_shape=[jax.ShapeDtypeStruct((heads, seq_len, head_dim), jnp.bfloat16)] * 3,
        compiler_params=params(),
        cost_estimate=SHORT,
        name="project",
    )(rows, weights, cosine, sine)


def cotangent_kernel(scale, rows_ref, weight_ref, out_ref):
    heads, head_dim, width = weight_ref.shape
    some = math.gcd(heads, 2)

    def of_heads(index, carry):
        first = index * some
        weights = weight_ref[pl.ds(first, some)].reshape(some * head_dim, width)
        grads = (product(rows_ref[...], weights, 1, 1) * scale).astype(jnp.bfloat16)
        for number in range(some):
            out_ref[first + number] = grads[:, number * head_dim : (number + 1) * head_dim]
        return carry

    lax.fori_loop(0, heads // some, of_heads, 0)


def cotangent(rows, weights, scale):
    seq_len, width = rows.shape
    heads, head_dim, _ = weights.shape
    block = min(BLOCK, seq_len)
    return pl.pallas_call(
        partial(cotangent_kernel, scale),
        grid=(seq_len // block,),
        in_specs=[
            pl.BlockSpec((block, width), lambda i: (i, 0)),
            pl.BlockSpec((heads, head_dim, width), lambda i: (0, 0, 0)),
        ],
        out_specs=pl.BlockSpec((heads, block, head_dim), lambda i: (0, i, 0)),
        out_shape=jax.ShapeDtypeStruct((heads, seq_len, head_dim), jnp.bfloat16),
        compiler_params=params(),
        cost_estimate=SHORT,
        name="cotangent",
    )(rows, weights)


def folded(values, combine):
    rows, columns = values.shape
    return combine(values.reshape(rows // 8, 8, columns), 0)


def attention_kernel(
    scale,
    proj_scale,
    q_ref,
    k_ref,
    v_ref,
    g_ref,
    cos_ref,
    sin_ref,
    grad_ref,
    att_ref,
    s_ref,
    p_ref,
    d_ref,
    kt_ref,
    vt_ref,
    gk_ref,
    gv_ref,
):
    step = pl.program_id(1)
    _, tile_len, block = s_ref.shape
    head_dim = q_ref.shape[-1]
    half = head_dim // 2
    in_block = block // tile_len

    def rows(tile):
        return pl.ds(pl.multiple_of(tile * tile_len, tile_len), tile_len)

    here = pl.ds(pl.multiple_of(step * block, block), block)
    queries = q_ref[0, here, :]
    grads = g_ref[0, here, :]
    first_tile, tiles = step * in_block, (step + 1) * in_block

    def enter(tile, carry):
        kt_ref[tile] = k_ref[0, rows(tile), :].T
        vt_ref[tile] = v_ref[0, rows(tile), :].T
        gk_ref[tile] = jnp.zeros(gk_ref.shape[1:], jnp.float32)
        gv_ref[tile] = jnp.zeros(gv_ref.shape[1:], jnp.float32)
        return carry

    lax.fori_loop(first_tile, tiles, enter, 0)

    behind = lax.broadcasted_iota(jnp.int32, (tile_len, block), 0) - lax.broadcasted_iota(
        jnp.int32, (tile_len, block), 1
    )

    def score(tile, top):
        scores = product(k_ref[0, rows(tile), :], queries, 1, 1)
        scores = jnp.where(behind <= step * block - tile * tile_len, scores, -jnp.inf)
        s_ref[tile] = scores
        return jnp.maximum(top, folded(scores, jnp.max))

    top = lax.fori_loop(0, tiles, score, jnp.full((8, block), -jnp.inf, jnp.float32))
    factor = scale * math.log2(math.e)
    top = jnp.max(top, 0, keepdims=True) * factor

    def weigh(tile, sums):
        total, inner = sums
        weights = jnp.exp2(s_ref[tile] * factor - top)
        grad_probs = product(v_ref[0, rows(tile), :], grads, 1, 1)
        p_ref[tile] = weights
        d_ref[tile] = grad_probs
        return total + folded(weights, jnp.sum), inner + folded(weights * grad_probs, jnp.sum)

    zeros = jnp.zeros((8, block), jnp.float32)
    total, inner = lax.fori_loop(0, tiles, weigh, (zeros, zeros))
    inverse = 1.0 / jnp.sum(total, 0, keepdims=True)
    inner = jnp.sum(inner, 0, keepdims=True) * inverse

    def back(tile, sums):
        att, grad_q = sums
        probs = p_ref[tile] * inverse
        probs_b = probs.astype(jnp.bfloat16)
        grad_scores = (probs * (d_ref[tile] - inner)).astype(jnp.bfloat16)
        gv_ref[tile] += product(probs_b, grads)
        gk_ref[tile] += product(grad_scores, queries)
        return att + product(vt_ref[tile], probs_b), grad_q + product(kt_ref[tile], grad_scores)

    zeros = jnp.zeros((head_dim, block), jnp.float32)
    att, grad_q = lax.fori_loop(0, tiles, back, (zeros, zeros))

    att_ref[0, :, here] = att.astype(jnp.bfloat16)
    cosine, sine = cos_ref[here, :].T, sin_ref[here, :].T
    turned = grad_q * cosine - pltpu.roll(grad_q, half, 0) * sine
    grad_ref[0, :head_dim, here] = (turned * (scale * proj_scale)).astype(jnp.bfloat16)

    @pl.when(step == pl.num_programs(1) - 1)
    def finish():
        def keys(tile, carry):
            where = rows(tile)
            grad_k = gk_ref[tile]
            turned = grad_k * cos_ref[where, :] - pltpu.roll(grad_k, half, 1) * sin_ref[where, :]
            turned = (turned * (scale * proj_scale)).T
            grad_ref[0, head_dim : 2 * head_dim, where] = turned.astype(jnp.bfloat16)
            values = gv_ref[tile].T * proj_scale
            grad_ref[0, 2 * head_dim :, where] = values.astype(jnp.bfloat16)
            return carry

        lax.fori_loop(0, tiles, keys, 0)


def attention(group, queries, keys, values, grads, cosine, sine, width):
    first, count = group
    _, seq_len, head_dim = queries.shape
    block = min(BLOCK, seq_len)
    tile_len = min(TILE, block)
    tiles = seq_len // tile_len
    of_head = pl.BlockSpec((1, seq_len, head_dim), lambda h, i: (first + h, 0, 0))
    table = pl.BlockSpec((seq_len, head_dim), lambda h, i: (0, 0))
    return pl.pallas_call(
        partial(attention_kernel, 1.0 / math.sqrt(head_dim), 1.0 / math.sqrt(width)),
        grid=(count, seq_len // block),
        in_specs=[of_head] * 4 + [table] * 2,
        out_specs=[
            pl.BlockSpec((1, 3 * head_dim, seq_len), lambda h, i: (h, 0, 0)),
            pl.BlockSpec((1, head_dim, seq_len), lambda h, i: (h, 0, 0)),
        ],
        out_shape=[
            jax.ShapeDtypeStruct((count, 3 * head_dim, seq_len), jnp.bfloat16),
            jax.ShapeDtypeStruct((count, head_dim, seq_len), jnp.bfloat16),
        ],
        scratch_shapes=[pltpu.VMEM((tiles, tile_len, block), jnp.float32)] * 3
        + [pltpu.VMEM((tiles, head_dim, tile_len), jnp.bfloat16)] * 2
        + [pltpu.VMEM((tiles, tile_len, head_dim), jnp.float32)] * 2,
        compiler_params=params(),
        cost_estimate=SHORT,
        name="attention",
    )(queries, keys, values, grads, cosine, sine)


def momenta_kernel(
    scale, grad_ref, att_ref, normed_ref, rows_ref, mqkv_ref, mout_ref, *refs
):
    outs, moved_ref = refs[:-1], refs[-1]
    count, three, _ = grad_ref.shape

    def of_head(head, carry):
        def chunk(here):
            grad = product(grad_ref[head], normed_ref[:, here]).T.astype(jnp.bfloat16)
            moved = BETA * mqkv_ref[head, here, :].astype(jnp.float32) + grad.astype(jnp.float32)
            moved_ref[head, here, :three] = moved.astype(jnp.bfloat16)
            grad = (product(att_ref[head], rows_ref[:, here]) * scale).astype(jnp.bfloat16)
            moved = BETA * mout_ref[head, :, here].astype(jnp.float32) + grad.astype(jnp.float32)
            moved_ref[head, here, three:] = moved.T.astype(jnp.bfloat16)

        in_chunks(moved_ref.shape[1], CHUNK, chunk)
        return carry

    lax.fori_loop(0, count, of_head, 0)
    if not outs:
        return
    step, last, block = pl.program_id(0), pl.num_programs(0) - 1, moved_ref.shape[1]
    for out_ref, mine in zip(outs, (step < last, step == last)):

        @pl.when(mine)
        def hand_out(out_ref=out_ref):
            above = pl.multiple_of(step * block % out_ref.shape[1], block)

            def copy(here):
                place = pl.ds(pl.multiple_of(above + here.start, 32), here.size)
                out_ref[:, place, :] = moved_ref[:, here, :]

            in_chunks(block, 32, copy)


def momenta(group, piece, apart, grad_proj, attended, normed, rows, mom_qkv, mom_out, scale):
    first, count, block = piece
    start, heads = group
    seq_len = normed.shape[0]
    three, head_dim = grad_proj.shape[1], attended.shape[1]
    group_index = start // heads
    packed = (heads, block, three + head_dim)
    if apart:
        parts = [(heads, high, packed[-1]) for high in ((count - 1) * block, block)]
        out_specs = [pl.BlockSpec(part, lambda i: (0, 0, 0)) for part in parts]
        out_shape = [jax.ShapeDtypeStruct(part, jnp.bfloat16) for part in parts]
    else:
        out_specs = pl.BlockSpec(packed, lambda i: (0, i, 0))
        out_shape = jax.ShapeDtypeStruct((heads, count * block, packed[-1]), jnp.bfloat16)
    return pl.pallas_call(
        partial(momenta_kernel, scale),
        grid=(count,),
        in_specs=[
            pl.BlockSpec((heads, three, seq_len), lambda i: (0, 0, 0)),
            pl.BlockSpec((heads, head_dim, seq_len), lambda i: (0, 0, 0)),
            pl.BlockSpec((seq_len, block), lambda i: (0, first + i)),
            pl.BlockSpec((seq_len, block), lambda i: (0, first + i)),
            pl.BlockSpec((heads, block, three), lambda i: (group_index, first + i, 0)),
            pl.BlockSpec((heads, head_dim, block), lambda i: (group_index, 0, first + i)),
        ],
        out_specs=out_specs,
        out_shape=out_shape,
        scratch_shapes=[pltpu.VMEM(packed, jnp.bfloat16)] if apart else [],
        compiler_params=params(),
        cost_estimate=SHORT,
        name="momenta",
    )(grad_proj, attended, normed, rows, mom_qkv, mom_out)


def average_kernel(rate_ref, qkv, other_qkv, out, other_out, moment, other_moment, *refs):
    rate = rate_ref[0, 0]
    new_qkv, new_out, new_mom_qkv, new_mom_out = refs[-4:]
    three = qkv.shape[-1]

    def halfway(own, other):
        return ((own.astype(jnp.float32) + other.astype(jnp.float32)) * 0.5).astype(jnp.bfloat16)

    def moved(weight, moment):
        new = weight.astype(jnp.float32) - rate * moment.astype(jnp.float32)
        return new.astype(jnp.bfloat16)

    def chunk(here):
        own, other = moment[0, here, :three], other_moment[0, here, :three]
        new = halfway(moved(qkv[0, 0, here, :], own), moved(other_qkv[0, 0, here, :], other))
        new_qkv[0, 0, here, :] = new
        new_mom_qkv[0, 0, here, :] = halfway(own, other)
        own = moment[0, here, three:].T
        other = other_moment[0, here, three:].T
        new = halfway(moved(out[0, 0, :, here], own), moved(other_out[0, 0, :, here], other))
        new_out[0, 0, :, here] = new
        new_mom_out[0, 0, :, here] = halfway(own, other)

    in_chunks(moment.shape[1], 128, chunk)


def average(group, piece, rate, own, other, moment, other_moment, previous):
    first, count, block = piece
    start, heads = group
    (qkv, out), (other_qkv, other_out) = own, other
    three, head_dim = qkv.shape[-1], out.shape[2]
    high = pl.BlockSpec((1, 1, block, three), lambda h, i: (0, start + h, first + i, 0))
    wide = pl.BlockSpec((1, 1, head_dim, block), lambda h, i: (0, start + h, 0, first + i))
    packed = pl.BlockSpec((1, block, three + head_dim), lambda h, i: (h, i, 0))
    in_specs = [pl.BlockSpec(memory_space=pltpu.SMEM), high, high, wide, wide, packed, packed]
    args = [rate, qkv, other_qkv, out, other_out, moment, other_moment]
    aliases = {}
    if previous is not None:
        aliases = {len(args) + i: i for i in range(4)}
        args += list(previous)
        in_specs += [pl.BlockSpec(memory_space=pl.ANY)] * 4
    return pl.pallas_call(
        average_kernel,
        grid=(heads, count),
        in_specs=in_specs,
        out_specs=[high, wide] * 2,
        out_shape=[jax.ShapeDtypeStruct(w.shape, jnp.bfloat16) for w in own] * 2,
        input_output_aliases=aliases,
        compiler_params=params(),
        cost_estimate=SHORT,
        name="average",
    )(*args)


def pieces_of(last, width):
    if not last or width % BLOCK or width < 2 * BLOCK:
        block = min(BLOCK, width)
        return [(0, width // block, block, False)]
    small = BLOCK // 4
    return [(0, width // BLOCK - 1, BLOCK, False), (width // small - 4, 4, small, True)]


def update(by, inputs, out_grad, norm_gain, w_qkv, w_out, mom_qkv, mom_out, rate):
    own = (w_qkv, w_out)
    other_qkv = shifted(w_qkv, by)

    devices = lax.axis_size("fsdp")
    blocks = exchanged([normalised(inputs, norm_gain, part) for part in range(PARTS)], 0)
    row_blocks = exchanged([out_grad], 0)
    stage = 1
    while len(blocks) < devices * PARTS:
        blocks = exchanged(blocks, stage)
        stage += 1
    normed = assembled(blocks)
    other_out = shifted(w_out, by)
    w_qkv, w_out = w_qkv[0], w_out[0]

    seq_len, width = normed.shape
    heads, head_dim, _ = w_out.shape
    out_scale = 1.0 / math.sqrt(HEADS * head_dim)
    tables = rotary_tables(seq_len, head_dim)
    parts = project(normed, w_qkv, *tables)
    row_blocks[-1], parts = lax.optimization_barrier((row_blocks[-1], parts))
    stage = 1
    while len(row_blocks) < devices:
        row_blocks = exchanged(row_blocks, stage)
        stage += 1
    rows = assembled(row_blocks)
    grads = cotangent(rows, w_out, out_scale)

    made = []
    some = max(heads // 2, 1)
    for start in range(0, heads, some):
        group = (start, some)
        grad_proj, attended = attention(group, *parts, grads, *tables, width)
        if start == 0:
            grad_proj, other_qkv = lax.optimization_barrier((grad_proj, other_qkv))
        if start + some == heads:
            grad_proj, other_out = lax.optimization_barrier((grad_proj, other_out))
        for first, count, block, apart in pieces_of(start + some == heads, width):
            piece = (first, count, block)
            moment = momenta(
                group, piece, apart, grad_proj, attended, normed, rows, mom_qkv, mom_out, out_scale
            )
            grads, normed, moment = lax.optimization_barrier((grads, normed, moment))
            if apart:
                places = ((first, count - 1, block), (first + count - 1, 1, block))
                for place, part in zip(places, moment):
                    made.append((group, place, part, shifted(part, by)))
            else:
                made.append((group, piece, moment, shifted(moment, by)))
    results, other = None, (other_qkv, other_out)
    for group, piece, moment, other_moment in made:
        results = average(group, piece, rate, own, other, moment, other_moment, results)
    return tuple(results)


def per_device(inputs, out_grad, norm_gain, w_qkv, w_out, mom_qkv, mom_out, step_index):
    rate = RATE * (step_index[0].astype(jnp.float32) + 1.0) / (4.0 * LEVELS)
    exponent = jnp.remainder(step_index[0], LEVELS)
    return lax.switch(
        exponent,
        [partial(update, 1 << level) for level in range(LEVELS)],
        inputs[0],
        out_grad[0],
        norm_gain,
        w_qkv,
        w_out,
        mom_qkv[0],
        mom_out[0],
        rate.reshape(1, 1),
    )


def solution(mesh):
    return jax.shard_map(
        per_device,
        mesh=mesh,
        in_specs=(
            P("gossip", "fsdp", None),
            P("gossip", "fsdp", None),
            P("gossip", None),
            P("gossip", "fsdp", None, None),
            P("gossip", "fsdp", None, None),
            P("gossip", "fsdp", None, None),
            P("gossip", "fsdp", None, None),
            P(),
        ),
        out_specs=(
            P("gossip", "fsdp", None, None),
            P("gossip", "fsdp", None, None),
            P("gossip", "fsdp", None, None),
            P("gossip", "fsdp", None, None),
        ),
        check_vma=False,
    )
```

```python
from functools import partial
import math

import jax
import jax.numpy as jnp
from jax import lax
from jax.experimental import pallas as pl
from jax.experimental.pallas import tpu as pltpu
from jax.sharding import PartitionSpec as P

HEADS = 16
LEVELS = 3

BETA = 0.9
RATE = 0.1
EPSILON = 1e-05

VMEM_LIMIT = 65408 * 1024
BLOCK = 512
CHUNK = 256
TILE = 512
PARTS = 2

SHORT = pl.CostEstimate(flops=1, bytes_accessed=1, transcendentals=0)


def product(left, right, left_dim=1, right_dim=0):
    return lax.dot_general(
        left, right, (((left_dim,), (right_dim,)), ((), ())), preferred_element_type=jnp.float32
    )


def in_chunks(size, chunk, body):
    chunk = min(chunk, size)

    def step(index, carry):
        body(pl.ds(pl.multiple_of(index * chunk, chunk), chunk))
        return carry

    lax.fori_loop(0, size // chunk, step, 0)


def params():
    return pltpu.CompilerParams(vmem_limit_bytes=VMEM_LIMIT)


def shifted(value, by):
    size = lax.axis_size("gossip")
    return lax.ppermute(value, "gossip", [(i, (i + by) % size) for i in range(size)])


def exchanged(blocks, stage):
    size = lax.axis_size("fsdp")
    bit = size >> (stage + 1)
    pairs = [(i, i ^ bit) for i in range(size)]
    return blocks + [lax.ppermute(block, "fsdp", pairs) for block in blocks]


def places_of(size, parts):
    places, bit = [(0, part) for part in range(parts)], size // 2
    while bit:
        places += [(offset ^ bit, part) for offset, part in places]
        bit //= 2
    return places


def assemble_kernel(places, *refs):
    blocks, (out_ref, held, came, left) = refs[:-4], refs[-4:]
    me = lax.axis_index("fsdp")
    high = blocks[0].shape[0]
    inward, outward = [], []
    parts = 1 + max(part for _, part in places)
    for number, ((offset, part), block) in enumerate(zip(places, blocks)):
        place = pl.ds(pl.multiple_of(((me ^ offset) * parts + part) * high, high), high)
        inward.append(pltpu.make_async_copy(block, held.at[number], came.at[number]))
        outward.append(
            pltpu.make_async_copy(held.at[number], out_ref.at[place, :], left.at[number])
        )
        inward[-1].start()
    for first, second in zip(inward, outward):
        first.wait()
        second.start()
    for copy in outward:
        copy.wait()


def assembled(blocks):
    size, devices = len(blocks), lax.axis_size("fsdp")
    high, wide = blocks[0].shape
    return pl.pallas_call(
        partial(assemble_kernel, places_of(devices, size // devices)),
        in_specs=[pl.BlockSpec(memory_space=pl.ANY)] * size,
        out_specs=pl.BlockSpec(memory_space=pl.ANY),
        out_shape=jax.ShapeDtypeStruct((size * high, wide), blocks[0].dtype),
        scratch_shapes=[
            pltpu.VMEM((size, high, wide), blocks[0].dtype),
            pltpu.SemaphoreType.DMA((size,)),
            pltpu.SemaphoreType.DMA((size,)),
        ],
        compiler_params=params(),
        cost_estimate=SHORT,
        name="assemble",
    )(*blocks)


def rotary_tables(seq_len, head_dim):
    half = head_dim // 2
    column = jnp.arange(head_dim)
    frequency = jnp.exp(
        -math.log(10000.0) * 2.0 * (column % half).astype(jnp.float32) / head_dim
    )
    angles = jnp.arange(seq_len).astype(jnp.float32)[:, None] * frequency[None, :]
    sign = jnp.where(column < half, -1.0, 1.0)
    return jnp.cos(angles), jnp.sin(angles) * sign[None, :]


def norm_kernel(rows_ref, gain_ref, out_ref):
    def chunk(here):
        rows = rows_ref[here, :].astype(jnp.float32)
        stats = lax.rsqrt(jnp.mean(rows * rows, -1, keepdims=True) + EPSILON)
        out_ref[here, :] = (rows * stats * gain_ref[...]).astype(jnp.bfloat16)

    in_chunks(rows_ref.shape[0], 64, chunk)


def normalised(rows, gain, part):
    high, wide = rows.shape
    block = high // PARTS
    return pl.pallas_call(
        norm_kernel,
        grid=(1,),
        in_specs=[
            pl.BlockSpec((block, wide), lambda i: (part, 0)),
            pl.BlockSpec((1, wide), lambda i: (0, 0)),
        ],
        out_specs=pl.BlockSpec((block, wide), lambda i: (0, 0)),
        out_shape=jax.ShapeDtypeStruct((block, wide), jnp.bfloat16),
        compiler_params=params(),
        cost_estimate=SHORT,
        name="normalised",
    )(rows, gain)


def project_kernel(scale, rows_ref, weight_ref, cos_ref, sin_ref, q_ref, k_ref, v_ref):
    width = cos_ref.shape[-1]

    def of_head(head, carry):
        def chunk(here):
            cosine, sine = cos_ref[here, :], sin_ref[here, :]
            projected = product(rows_ref[here, :], weight_ref[head]) * scale
            for which, out_ref in enumerate((q_ref, k_ref)):
                part = projected[:, which * width : (which + 1) * width]
                turned = part * cosine + pltpu.roll(part, width // 2, 1) * sine
                out_ref[head, here, :] = turned.astype(jnp.bfloat16)
            v_ref[head, here, :] = projected[:, 2 * width :].astype(jnp.bfloat16)

        in_chunks(rows_ref.shape[0], CHUNK, chunk)
        return carry

    lax.fori_loop(0, weight_ref.shape[0], of_head, 0)


def project(rows, weights, cosine, sine):
    seq_len, width = rows.shape
    heads, _, three = weights.shape
    head_dim = three // 3
    block = min(BLOCK, seq_len)
    table = pl.BlockSpec((block, head_dim), lambda i: (i, 0))
    return pl.pallas_call(
        partial(project_kernel, 1.0 / math.sqrt(width)),
        grid=(seq_len // block,),
        in_specs=[
            pl.BlockSpec((block, width), lambda i: (i, 0)),
            pl.BlockSpec((heads, width, three), lambda i: (0, 0, 0)),
            table,
            table,
        ],
        out_specs=[pl.BlockSpec((heads, block, head_dim), lambda i: (0, i, 0))] * 3,
        out_shape=[jax.ShapeDtypeStruct((heads, seq_len, head_dim), jnp.bfloat16)] * 3,
        compiler_params=params(),
        cost_estimate=SHORT,
        name="project",
    )(rows, weights, cosine, sine)


def cotangent_kernel(scale, rows_ref, weight_ref, out_ref):
    heads, head_dim, width = weight_ref.shape
    some = math.gcd(heads, 2)

    def of_heads(index, carry):
        first = index * some
        weights = weight_ref[pl.ds(first, some)].reshape(some * head_dim, width)
        grads = (product(rows_ref[...], weights, 1, 1) * scale).astype(jnp.bfloat16)
        for number in range(some):
            out_ref[first + number] = grads[:, number * head_dim : (number + 1) * head_dim]
        return carry

    lax.fori_loop(0, heads // some, of_heads, 0)


def cotangent(rows, weights, scale):
    seq_len, width = rows.shape
    heads, head_dim, _ = weights.shape
    block = min(BLOCK, seq_len)
    return pl.pallas_call(
        partial(cotangent_kernel, scale),
        grid=(seq_len // block,),
        in_specs=[
            pl.BlockSpec((block, width), lambda i: (i, 0)),
            pl.BlockSpec((heads, head_dim, width), lambda i: (0, 0, 0)),
        ],
        out_specs=pl.BlockSpec((heads, block, head_dim), lambda i: (0, i, 0)),
        out_shape=jax.ShapeDtypeStruct((heads, seq_len, head_dim), jnp.bfloat16),
        compiler_params=params(),
        cost_estimate=SHORT,
        name="cotangent",
    )(rows, weights)


def folded(values, combine):
    rows, columns = values.shape
    return combine(values.reshape(rows // 8, 8, columns), 0)


def attention_kernel(
    scale,
    proj_scale,
    q_ref,
    k_ref,
    v_ref,
    g_ref,
    cos_ref,
    sin_ref,
    grad_ref,
    att_ref,
    s_ref,
    p_ref,
    d_ref,
    kt_ref,
    vt_ref,
    gk_ref,
    gv_ref,
):
    step = pl.program_id(1)
    _, tile_len, block = s_ref.shape
    head_dim = q_ref.shape[-1]
    half = head_dim // 2
    in_block = block // tile_len

    def rows(tile):
        return pl.ds(pl.multiple_of(tile * tile_len, tile_len), tile_len)

    here = pl.ds(pl.multiple_of(step * block, block), block)
    queries = q_ref[0, here, :]
    grads = g_ref[0, here, :]
    first_tile, tiles = step * in_block, (step + 1) * in_block

    def enter(tile, carry):
        kt_ref[tile] = k_ref[0, rows(tile), :].T
        vt_ref[tile] = v_ref[0, rows(tile), :].T
        gk_ref[tile] = jnp.zeros(gk_ref.shape[1:], jnp.float32)
        gv_ref[tile] = jnp.zeros(gv_ref.shape[1:], jnp.float32)
        return carry

    lax.fori_loop(first_tile, tiles, enter, 0)

    behind = lax.broadcasted_iota(jnp.int32, (tile_len, block), 0) - lax.broadcasted_iota(
        jnp.int32, (tile_len, block), 1
    )

    def score(tile, top):
        scores = product(k_ref[0, rows(tile), :], queries, 1, 1)
        scores = jnp.where(behind <= step * block - tile * tile_len, scores, -jnp.inf)
        s_ref[tile] = scores
        return jnp.maximum(top, folded(scores, jnp.max))

    top = lax.fori_loop(0, tiles, score, jnp.full((8, block), -jnp.inf, jnp.float32))
    factor = scale * math.log2(math.e)
    top = jnp.max(top, 0, keepdims=True) * factor

    def weigh(tile, sums):
        total, inner = sums
        weights = jnp.exp2(s_ref[tile] * factor - top)
        grad_probs = product(v_ref[0, rows(tile), :], grads, 1, 1)
        p_ref[tile] = weights
        d_ref[tile] = grad_probs
        return total + folded(weights, jnp.sum), inner + folded(weights * grad_probs, jnp.sum)

    zeros = jnp.zeros((8, block), jnp.float32)
    total, inner = lax.fori_loop(0, tiles, weigh, (zeros, zeros))
    inverse = 1.0 / jnp.sum(total, 0, keepdims=True)
    inner = jnp.sum(inner, 0, keepdims=True) * inverse

    def back(tile, sums):
        att, grad_q = sums
        probs = p_ref[tile] * inverse
        probs_b = probs.astype(jnp.bfloat16)
        grad_scores = (probs * (d_ref[tile] - inner)).astype(jnp.bfloat16)
        gv_ref[tile] += product(probs_b, grads)
        gk_ref[tile] += product(grad_scores, queries)
        return att + product(vt_ref[tile], probs_b), grad_q + product(kt_ref[tile], grad_scores)

    zeros = jnp.zeros((head_dim, block), jnp.float32)
    att, grad_q = lax.fori_loop(0, tiles, back, (zeros, zeros))

    att_ref[0, :, here] = att.astype(jnp.bfloat16)
    cosine, sine = cos_ref[here, :].T, sin_ref[here, :].T
    turned = grad_q * cosine - pltpu.roll(grad_q, half, 0) * sine
    grad_ref[0, :head_dim, here] = (turned * (scale * proj_scale)).astype(jnp.bfloat16)

    @pl.when(step == pl.num_programs(1) - 1)
    def finish():
        def keys(tile, carry):
            where = rows(tile)
            grad_k = gk_ref[tile]
            turned = grad_k * cos_ref[where, :] - pltpu.roll(grad_k, half, 1) * sin_ref[where, :]
            turned = (turned * (scale * proj_scale)).T
            grad_ref[0, head_dim : 2 * head_dim, where] = turned.astype(jnp.bfloat16)
            values = gv_ref[tile].T * proj_scale
            grad_ref[0, 2 * head_dim :, where] = values.astype(jnp.bfloat16)
            return carry

        lax.fori_loop(0, tiles, keys, 0)


def attention(group, queries, keys, values, grads, cosine, sine, width):
    first, count = group
    _, seq_len, head_dim = queries.shape
    block = min(BLOCK, seq_len)
    tile_len = min(TILE, block)
    tiles = seq_len // tile_len
    of_head = pl.BlockSpec((1, seq_len, head_dim), lambda h, i: (first + h, 0, 0))
    table = pl.BlockSpec((seq_len, head_dim), lambda h, i: (0, 0))
    return pl.pallas_call(
        partial(attention_kernel, 1.0 / math.sqrt(head_dim), 1.0 / math.sqrt(width)),
        grid=(count, seq_len // block),
        in_specs=[of_head] * 4 + [table] * 2,
        out_specs=[
            pl.BlockSpec((1, 3 * head_dim, seq_len), lambda h, i: (h, 0, 0)),
            pl.BlockSpec((1, head_dim, seq_len), lambda h, i: (h, 0, 0)),
        ],
        out_shape=[
            jax.ShapeDtypeStruct((count, 3 * head_dim, seq_len), jnp.bfloat16),
            jax.ShapeDtypeStruct((count, head_dim, seq_len), jnp.bfloat16),
        ],
        scratch_shapes=[pltpu.VMEM((tiles, tile_len, block), jnp.float32)] * 3
        + [pltpu.VMEM((tiles, head_dim, tile_len), jnp.bfloat16)] * 2
        + [pltpu.VMEM((tiles, tile_len, head_dim), jnp.float32)] * 2,
        compiler_params=params(),
        cost_estimate=SHORT,
        name="attention",
    )(queries, keys, values, grads, cosine, sine)


def momenta_kernel(
    scale, grad_ref, att_ref, normed_ref, rows_ref, mqkv_ref, mout_ref, *refs
):
    outs, moved_ref = refs[:-1], refs[-1]
    count, three, _ = grad_ref.shape

    def of_head(head, carry):
        def chunk(here):
            grad = product(grad_ref[head], normed_ref[:, here]).T.astype(jnp.bfloat16)
            moved = BETA * mqkv_ref[head, here, :].astype(jnp.float32) + grad.astype(jnp.float32)
            moved_ref[head, here, :three] = moved.astype(jnp.bfloat16)
            grad = (product(att_ref[head], rows_ref[:, here]) * scale).astype(jnp.bfloat16)
            moved = BETA * mout_ref[head, :, here].astype(jnp.float32) + grad.astype(jnp.float32)
            moved_ref[head, here, three:] = moved.T.astype(jnp.bfloat16)

        in_chunks(moved_ref.shape[1], CHUNK, chunk)
        return carry

    lax.fori_loop(0, count, of_head, 0)
    if not outs:
        return
    step, last, block = pl.program_id(0), pl.num_programs(0) - 1, moved_ref.shape[1]
    for out_ref, mine in zip(outs, (step < last, step == last)):

        @pl.when(mine)
        def hand_out(out_ref=out_ref):
            above = pl.multiple_of(step * block % out_ref.shape[1], block)

            def copy(here):
                place = pl.ds(pl.multiple_of(above + here.start, 32), here.size)
                out_ref[:, place, :] = moved_ref[:, here, :]

            in_chunks(block, 32, copy)


def momenta(group, piece, apart, grad_proj, attended, normed, rows, mom_qkv, mom_out, scale):
    first, count, block = piece
    start, heads = group
    seq_len = normed.shape[0]
    three, head_dim = grad_proj.shape[1], attended.shape[1]
    group_index = start // heads
    packed = (heads, block, three + head_dim)
    if apart:
        parts = [(heads, high, packed[-1]) for high in ((count - 1) * block, block)]
        out_specs = [pl.BlockSpec(part, lambda i: (0, 0, 0)) for part in parts]
        out_shape = [jax.ShapeDtypeStruct(part, jnp.bfloat16) for part in parts]
    else:
        out_specs = pl.BlockSpec(packed, lambda i: (0, i, 0))
        out_shape = jax.ShapeDtypeStruct((heads, count * block, packed[-1]), jnp.bfloat16)
    return pl.pallas_call(
        partial(momenta_kernel, scale),
        grid=(count,),
        in_specs=[
            pl.BlockSpec((heads, three, seq_len), lambda i: (0, 0, 0)),
            pl.BlockSpec((heads, head_dim, seq_len), lambda i: (0, 0, 0)),
            pl.BlockSpec((seq_len, block), lambda i: (0, first + i)),
            pl.BlockSpec((seq_len, block), lambda i: (0, first + i)),
            pl.BlockSpec((heads, block, three), lambda i: (group_index, first + i, 0)),
            pl.BlockSpec((heads, head_dim, block), lambda i: (group_index, 0, first + i)),
        ],
        out_specs=out_specs,
        out_shape=out_shape,
        scratch_shapes=[pltpu.VMEM(packed, jnp.bfloat16)] if apart else [],
        compiler_params=params(),
        cost_estimate=SHORT,
        name="momenta",
    )(grad_proj, attended, normed, rows, mom_qkv, mom_out)


def average_kernel(rate_ref, qkv, other_qkv, out, other_out, moment, other_moment, *refs):
    rate = rate_ref[0, 0]
    new_qkv, new_out, new_mom_qkv, new_mom_out = refs[-4:]
    three = qkv.shape[-1]

    def halfway(own, other):
        return ((own.astype(jnp.float32) + other.astype(jnp.float32)) * 0.5).astype(jnp.bfloat16)

    def moved(weight, moment):
        new = weight.astype(jnp.float32) - rate * moment.astype(jnp.float32)
        return new.astype(jnp.bfloat16)

    def chunk(here):
        own, other = moment[0, here, :three], other_moment[0, here, :three]
        new = halfway(moved(qkv[0, 0, here, :], own), moved(other_qkv[0, 0, here, :], other))
        new_qkv[0, 0, here, :] = new
        new_mom_qkv[0, 0, here, :] = halfway(own, other)
        own = moment[0, here, three:].T
        other = other_moment[0, here, three:].T
        new = halfway(moved(out[0, 0, :, here], own), moved(other_out[0, 0, :, here], other))
        new_out[0, 0, :, here] = new
        new_mom_out[0, 0, :, here] = halfway(own, other)

    in_chunks(moment.shape[1], 128, chunk)


def average(group, piece, rate, own, other, moment, other_moment, previous):
    first, count, block = piece
    start, heads = group
    (qkv, out), (other_qkv, other_out) = own, other
    three, head_dim = qkv.shape[-1], out.shape[2]
    high = pl.BlockSpec((1, 1, block, three), lambda h, i: (0, start + h, first + i, 0))
    wide = pl.BlockSpec((1, 1, head_dim, block), lambda h, i: (0, start + h, 0, first + i))
    packed = pl.BlockSpec((1, block, three + head_dim), lambda h, i: (h, i, 0))
    in_specs = [pl.BlockSpec(memory_space=pltpu.SMEM), high, high, wide, wide, packed, packed]
    args = [rate, qkv, other_qkv, out, other_out, moment, other_moment]
    aliases = {}
    if previous is not None:
        aliases = {len(args) + i: i for i in range(4)}
        args += list(previous)
        in_specs += [pl.BlockSpec(memory_space=pl.ANY)] * 4
    return pl.pallas_call(
        average_kernel,
        grid=(heads, count),
        in_specs=in_specs,
        out_specs=[high, wide] * 2,
        out_shape=[jax.ShapeDtypeStruct(w.shape, jnp.bfloat16) for w in own] * 2,
        input_output_aliases=aliases,
        compiler_params=params(),
        cost_estimate=SHORT,
        name="average",
    )(*args)


def pieces_of(last, width):
    if not last or width % BLOCK or width < 2 * BLOCK:
        block = min(BLOCK, width)
        return [(0, width // block, block, False)]
    small = BLOCK // 4
    return [(0, width // BLOCK - 1, BLOCK, False), (width // small - 4, 4, small, True)]


def update(by, inputs, out_grad, norm_gain, w_qkv, w_out, mom_qkv, mom_out, rate):
    own = (w_qkv, w_out)
    other_qkv = shifted(w_qkv, by)

    devices = lax.axis_size("fsdp")
    blocks = exchanged([normalised(inputs, norm_gain, part) for part in range(PARTS)], 0)
    row_blocks = exchanged([out_grad], 0)
    stage = 1
    while len(blocks) < devices * PARTS:
        blocks = exchanged(blocks, stage)
        stage += 1
    normed = assembled(blocks)
    other_out = shifted(w_out, by)
    w_qkv, w_out = w_qkv[0], w_out[0]

    seq_len, width = normed.shape
    heads, head_dim, _ = w_out.shape
    out_scale = 1.0 / math.sqrt(HEADS * head_dim)
    tables = rotary_tables(seq_len, head_dim)
    parts = project(normed, w_qkv, *tables)
    row_blocks[-1], parts = lax.optimization_barrier((row_blocks[-1], parts))
    stage = 1
    while len(row_blocks) < devices:
        row_blocks = exchanged(row_blocks, stage)
        stage += 1
    rows = assembled(row_blocks)
    grads = cotangent(rows, w_out, out_scale)

    made = []
    some = max(heads // 2, 1)
    for start in range(0, heads, some):
        group = (start, some)
        grad_proj, attended = attention(group, *parts, grads, *tables, width)
        if start == 0:
            grad_proj, other_qkv = lax.optimization_barrier((grad_proj, other_qkv))
        if start + some == heads:
            grad_proj, other_out = lax.optimization_barrier((grad_proj, other_out))
        for first, count, block, apart in pieces_of(start + some == heads, width):
            piece = (first, count, block)
            moment = momenta(
                group, piece, apart, grad_proj, attended, normed, rows, mom_qkv, mom_out, out_scale
            )
            grads, normed, moment = lax.optimization_barrier((grads, normed, moment))
            if apart:
                high = count - 1
                places = ((first // high, 1, high * block), (first + high, 1, block))
                for place, part in zip(places, moment):
                    made.append((group, place, part, shifted(part, by)))
            else:
                made.append((group, piece, moment, shifted(moment, by)))
    results, other = None, (other_qkv, other_out)
    for group, piece, moment, other_moment in made:
        results = average(group, piece, rate, own, other, moment, other_moment, results)
    return tuple(results)


def per_device(inputs, out_grad, norm_gain, w_qkv, w_out, mom_qkv, mom_out, step_index):
    rate = RATE * (step_index[0].astype(jnp.float32) + 1.0) / (4.0 * LEVELS)
    exponent = jnp.remainder(step_index[0], LEVELS)
    return lax.switch(
        exponent,
        [partial(update, 1 << level) for level in range(LEVELS)],
        inputs[0],
        out_grad[0],
        norm_gain,
        w_qkv,
        w_out,
        mom_qkv[0],
        mom_out[0],
        rate.reshape(1, 1),
    )


def solution(mesh):
    return jax.shard_map(
        per_device,
        mesh=mesh,
        in_specs=(
            P("gossip", "fsdp", None),
            P("gossip", "fsdp", None),
            P("gossip", None),
            P("gossip", "fsdp", None, None),
            P("gossip", "fsdp", None, None),
            P("gossip", "fsdp", None, None),
            P("gossip", "fsdp", None, None),
            P(),
        ),
        out_specs=(
            P("gossip", "fsdp", None, None),
            P("gossip", "fsdp", None, None),
            P("gossip", "fsdp", None, None),
            P("gossip", "fsdp", None, None),
        ),
        check_vma=False,
    )
```
